128 devices in a mesh: lat: 8 (over z_hi, x), lon: 16 (over y, z_lo, core).
Axes of the slice: x: 4, y: 4, z: 4 (z_hi: 2, z_lo: 2; z = z_hi * 2 + z_lo), core: 2. Of those that a mesh axis runs over, the one named last changes fastest.
Arguments:
- fine_tokens: bfloat16 [8, 4, 48, 192, 512], P(None, None, 'lat', 'lon'), may hold values from -40 to 40
- gain_fine: float32 [512], replicated, may hold values from 0.1 to 1.9
- w_qkv_fine: bfloat16 [512, 1536], replicated, may hold values from -0.25 to 0.25
- bias_fine: float32 [8, 144, 144], replicated, may hold values from -4 to 220
- w_out_fine: bfloat16 [512, 512], replicated, may hold values from -0.25 to 0.25
- gain_merge: float32 [2048], replicated, may hold values from 0.1 to 1.9
- w_merge: bfloat16 [2048, 1024], replicated, may hold values from -0.125 to 0.125
- gain_coarse: float32 [1024], replicated, may hold values from 0.1 to 1.9
- w_qkv_coarse: bfloat16 [1024, 3072], replicated, may hold values from -0.1875 to 0.1875
- bias_coarse: float32 [16, 144, 144], replicated, may hold values from -4 to 220
- w_out_coarse: bfloat16 [1024, 1024], replicated, may hold values from -0.1875 to 0.1875
Outputs:
- fine_out: float32 [8, 4, 48, 192, 512], P(None, None, 'lat', 'lon')
- coarse_out: float32 [8, 4, 24, 96, 1024], P(None, None, 'lat', 'lon')
The draws below stay inside these ranges and needn't reach their ends.
All inputs are finite; a program needn't handle non-finite values.
Results may differ from the reference program's by a relative error of at most 0.012.
Values may be sent and summed in bfloat16 or wider, within the bound.
A program may use at most 192 MiB of HBM per device.

```python
import math
import jax
import jax.numpy as jnp
from jax import lax

D1 = 512
D2 = 1024
HS = 64
WLEV = 2
WLAT = 6
WLON = 12
LEVELS = 4
BATCH = 8
WIN = 144
NLAT = 48
NLON = 192


def draw_fine_tokens(key, part):
    key = jax.random.fold_in(key, 11)
    key_base, key_cols, key_rows = jax.random.split(key, 3)
    full_shape = (BATCH, LEVELS, NLAT, NLON, D1)
    col_scale = jnp.exp(jax.random.uniform(key_cols, (D1,), jnp.float32, math.log(0.3), math.log(3.0)))
    row_scale = jnp.exp(jax.random.uniform(key_rows, full_shape[:-1] + (1,), jnp.float32, math.log(0.3), math.log(3.0)))
    rough_part = jnp.clip(jax.random.normal(key_base, full_shape, jnp.float32), -4.0, 4.0)
    return (rough_part * row_scale * col_scale).astype(jnp.bfloat16)


def draw_bias_fine(key, part):
    key = jax.random.fold_in(key, 23)
    key_base = jax.random.fold_in(key, 0)
    head_count = D1 // HS
    values = jnp.clip(jax.random.normal(key_base, (head_count, WIN, WIN), jnp.float32), -4.0, 4.0)
    return values.astype(jnp.float32)


def draw_bias_coarse(key, part):
    key = jax.random.fold_in(key, 37)
    key_base = jax.random.fold_in(key, 0)
    head_count = D2 // HS
    values = jnp.clip(jax.random.normal(key_base, (head_count, WIN, WIN), jnp.float32), -4.0, 4.0)
    return values.astype(jnp.float32)


def gaussian(stream_key, shape, spread, reach, dtype=jnp.bfloat16):
    return jnp.clip(spread * jax.random.normal(stream_key, shape, jnp.float32), -reach, reach).astype(dtype)


def setup_inputs(seed: int = 0) -> dict:
    splits = jax.random.split(jax.random.key(seed), 12)
    return {
        "fine_tokens": draw_fine_tokens(jax.random.fold_in(splits[11], 71), 0),
        "gain_fine": jnp.clip(1.0 + 0.18 * jax.random.normal(splits[1], (D1,), jnp.float32), 0.1, 1.9),
        "w_qkv_fine": gaussian(splits[2], (D1, 3 * D1), D1 ** -0.5, 0.25),
        "bias_fine": draw_bias_fine(jax.random.fold_in(splits[11], 71), 0),
        "w_out_fine": gaussian(splits[4], (D1, D1), D1 ** -0.5, 0.25),
        "gain_merge": jnp.clip(1.0 + 0.18 * jax.random.normal(splits[5], (4 * D1,), jnp.float32), 0.1, 1.9),
        "w_merge": gaussian(splits[6], (4 * D1, D2), (4 * D1) ** -0.5, 0.125),
        "gain_coarse": jnp.clip(1.0 + 0.18 * jax.random.normal(splits[7], (D2,), jnp.float32), 0.1, 1.9),
        "w_qkv_coarse": gaussian(splits[8], (D2, 3 * D2), D2 ** -0.5, 0.1875),
        "bias_coarse": draw_bias_coarse(jax.random.fold_in(splits[11], 71), 0),
        "w_out_coarse": gaussian(splits[10], (D2, D2), D2 ** -0.5, 0.1875),
    }


EPS = 1e-05
NEG = -1e+30

def layer_norm(values, gain):
    values = values.astype(jnp.float32)
    average = lax.optimization_barrier(jnp.mean(values, axis=-1, keepdims=True))
    centred = values - average
    variance = lax.optimization_barrier(jnp.mean(centred * centred, axis=-1, keepdims=True))
    return centred * lax.rsqrt(variance + EPS) * gain

def to_windows(grid_values, lat_size, lon_size):
    level_count, lat_count, lon_count, channels = grid_values.shape
    blocks = grid_values.reshape(level_count // WLEV, WLEV, lat_count // lat_size, lat_size, lon_count // lon_size, lon_size, channels)
    blocks = blocks.transpose(0, 2, 4, 1, 3, 5, 6)
    return blocks.reshape(-1, WLEV * lat_size * lon_size, channels)

def from_windows(windows, level_count, lat_count, lon_count, lat_size, lon_size):
    channels = windows.shape[-1]
    blocks = windows.reshape(level_count // WLEV, lat_count // lat_size, lon_count // lon_size, WLEV, lat_size, lon_size, channels)
    blocks = blocks.transpose(0, 3, 1, 4, 2, 5, 6)
    return blocks.reshape(level_count, lat_count, lon_count, channels)

def attend(qkv, bias, mask_add, head_count):
    win_count, token_count, triple = qkv.shape
    model_width = triple // 3
    head_size = model_width // head_count
    sections = qkv.astype(jnp.float32).reshape(win_count, token_count, 3, head_count, head_size)
    scores = jnp.einsum('wqhd,wkhd->whqk', sections[:, :, 0], sections[:, :, 1]) * head_size ** (-0.5)
    scores = scores + bias[None] + mask_add
    attn_probs = jax.nn.softmax(scores, axis=-1).astype(jnp.bfloat16)
    attended = jnp.einsum('whqk,wkhd->wqhd', attn_probs.astype(jnp.float32), sections[:, :, 2])
    return attended.astype(jnp.bfloat16).reshape(win_count, token_count, model_width)

def fine_mask():
    lat_windows = NLAT // WLAT
    token_row = jnp.arange(WIN) // WLON % WLAT
    window_lat = jnp.arange(lat_windows)
    region = (window_lat[:, None] == lat_windows - 1) & (token_row[None, :] >= WLAT // 2)
    region = jnp.broadcast_to(region[None, :, None, :], (LEVELS // WLEV, lat_windows, NLON // WLON, WIN)).reshape(-1, WIN)
    same_region = region[:, :, None] == region[:, None, :]
    return jnp.where(same_region, 0.0, NEG).astype(jnp.float32)[:, None]

def reference(fine_tokens, gain_fine, w_qkv_fine, bias_fine, w_out_fine, gain_merge, w_merge, gain_coarse, w_qkv_coarse, bias_coarse, w_out_coarse):
    mask_add = fine_mask()
    zero_mask = jnp.zeros((1, 1, WIN, WIN), jnp.float32)

    def sample_block(sample):
        normed = layer_norm(sample, gain_fine).astype(jnp.bfloat16)
        rolled = jnp.roll(normed, (-(WLAT // 2), -(WLON // 2)), axis=(1, 2))
        qkv_fine = jnp.dot(to_windows(rolled, WLAT, WLON), w_qkv_fine, preferred_element_type=jnp.float32).astype(jnp.bfloat16)
        heads_fine = attend(qkv_fine, bias_fine, mask_add, D1 // HS)
        shifted = from_windows(heads_fine, LEVELS, NLAT, NLON, WLAT, WLON)
        restored = jnp.roll(shifted, (WLAT // 2, WLON // 2), axis=(1, 2))
        fine_block = sample.astype(jnp.float32) + jnp.dot(restored, w_out_fine, preferred_element_type=jnp.float32)
        merged = fine_block.reshape(LEVELS, NLAT // 2, 2, NLON // 2, 2, D1).transpose(0, 1, 3, 4, 2, 5)
        merged = merged.reshape(LEVELS, NLAT // 2, NLON // 2, 4 * D1)
        merged_norm = layer_norm(merged, gain_merge).astype(jnp.bfloat16)
        coarse_in = jnp.dot(merged_norm, w_merge, preferred_element_type=jnp.float32).astype(jnp.bfloat16)
        normed_coarse = layer_norm(coarse_in, gain_coarse).astype(jnp.bfloat16)
        qkv_coarse = jnp.dot(to_windows(normed_coarse, WLAT, WLON), w_qkv_coarse, preferred_element_type=jnp.float32).astype(jnp.bfloat16)
        heads_coarse = attend(qkv_coarse, bias_coarse, zero_mask, D2 // HS)
        coarse_grid = from_windows(heads_coarse, LEVELS, NLAT // 2, NLON // 2, WLAT, WLON)
        coarse_block = coarse_in.astype(jnp.float32) + jnp.dot(coarse_grid, w_out_coarse, preferred_element_type=jnp.float32)
        return (fine_block, coarse_block)
    fine_result, coarse_result = lax.map(sample_block, fine_tokens)
    return (fine_result, coarse_result)
```

```python
import functools

import jax
import jax.numpy as jnp
import numpy as np
from jax import lax
from jax.experimental import pallas as pl
from jax.experimental.pallas import tpu as pltpu
from jax.sharding import PartitionSpec as P

EPS = 1e-05
NEG = -1e30
ROWS, COLS, WLEV, HS = 6, 12, 2, 64
HALF_R, HALF_C = ROWS // 2, COLS // 2
WIN = WLEV * ROWS * COLS
QUART = WLEV * HALF_R * HALF_C
STEP = 32
PIECE = 48
NW = 4
CROWS = NW * QUART
NAT = WLEV * ROWS * 16
D1, D2 = 512, 1024
IN_TILE = (0, 1, 2, 3)
IN_WINDOW = (3, 2, 1, 0)
TO_QUART, TO_GROUP, TO_WIN, HEADS_GROUP, HEADS_NAT, FROM_WIN = range(6)
MESH = pl.DeviceIdType.MESH
VMEM_LIMIT = 58 * 1024 * 1024


def row_maps():
    maps = np.zeros((6, NW, 4 * PIECE, 4 * PIECE), np.float32)
    for w in range(NW):
        shift = 4 * w
        for lev in range(WLEV):
            for r in range(ROWS):
                for c in range(COLS):
                    nat = (lev * ROWS + r) * 16 + c
                    win = lev * ROWS * COLS + r * COLS + c
                    q = (r // HALF_R) * 2 + c // HALF_C
                    t = lev * 18 + (r % HALF_R) * HALF_C + c % HALF_C
                    qp = q * PIECE + shift + t
                    g = (c % 2) * 2 + r % 2
                    gp = g * PIECE + shift + lev * 18 + (r // 2) * HALF_C + c // 2
                    maps[TO_QUART, w, qp, nat] = 1
                    maps[TO_GROUP, w, gp, nat] = 1
                    maps[TO_WIN, w, win, qp] = 1
                    maps[HEADS_GROUP, w, gp, qp] = 1
                    maps[HEADS_NAT, w, nat, qp] = 1
                    maps[FROM_WIN, w, qp, win] = 1
    return maps


def spread_map():
    spread = np.zeros((NW * WLEV * HALF_R * 8, CROWS), np.float32)
    for block in range(NW * WLEV * HALF_R):
        for j in range(HALF_C):
            spread[block * 8 + j, block * HALF_C + j] = 1
    return spread


def dot(a, b):
    return jnp.dot(a, b, preferred_element_type=jnp.float32)


def dot_t(a, b):
    return lax.dot_general(a, b, (((1,), (1,)), ((), ())), preferred_element_type=jnp.float32)


def normed(values, gain):
    average = jnp.mean(values, axis=-1, keepdims=True)
    centred = values - average
    variance = jnp.mean(centred * centred, axis=-1, keepdims=True)
    return (centred * lax.rsqrt(variance + EPS) * gain).astype(jnp.bfloat16)


def assemble(piece):
    blocks = []
    for n in range(9):
        w, part = divmod(n, 2)
        if w == NW:
            w, part = NW - 1, 2
        block = piece(w)[part * 16 : part * 16 + 16]
        if part == 0 and w > 0:
            block = block + piece(w - 1)[32:48]
        blocks.append(block)
    return jnp.concatenate(blocks, axis=0)


def attend_pair(query, key, value, bias0, bias1):
    low = lax.broadcasted_iota(jnp.int32, (WIN, 128), 1) < HS
    one = jnp.ones((), jnp.bfloat16)
    zero = jnp.zeros((), jnp.bfloat16)
    results = []
    for side, bias in ((low, bias0), (jnp.logical_not(low), bias1)):
        scores = dot_t(jnp.where(side, query, zero), key) + bias
        top = jnp.max(scores, axis=-1, keepdims=True)
        probs = jnp.exp(scores - top).astype(jnp.bfloat16)
        results.append(dot(probs, jnp.where(side, value, one)))
    total = jnp.where(low, results[0], results[1])
    weight = pltpu.roll(jnp.where(low, results[1], results[0]), HS, 1)
    return (total / weight).astype(jnp.bfloat16)


def main_kernel(
    n_chunks,
    n_lat,
    n_lon,
    tokens_hbm,
    gain_fine,
    w_qkv_fine_hbm,
    bias_fine_hbm,
    w_out_fine_hbm,
    gain_merge,
    w_merge_hbm,
    gain_coarse,
    w_qkv_coarse_hbm,
    bias_coarse_hbm,
    maps_hbm,
    heads_nat_hbm,
    coarse_in_hbm,
    heads_coarse_hbm,
    tokens,
    w_qkv_fine,
    bias_fine,
    w_out_fine,
    w_merge,
    w_qkv_coarse,
    bias_coarse,
    maps,
    padded,
    pieces,
    fine_send,
    fine_recv,
    xn,
    qkv,
    heads_send,
    heads_recv,
    group_heads,
    fine_rows,
    heads_nat,
    coarse_in,
    coarse_recv,
    xn_coarse,
    qkv_coarse,
    back_send,
    back_recv,
    heads_coarse,
    load_sem,
    token_sem,
    fine_ssem,
    fine_rsem,
    heads_ssem,
    heads_rsem,
    coarse_ssem,
    coarse_rsem,
    back_ssem,
    back_rsem,
    out_sem,
):
    lat = lax.axis_index("lat")
    lon = lax.axis_index("lon")
    member = (lat % 2) * 2 + lon % 2

    def at(dlat, dlon):
        return (lax.rem(lat + dlat + n_lat, n_lat), lax.rem(lon + dlon + n_lon, n_lon))

    def partner(k):
        return (
            lat + (k // 2) * (1 - 2 * (lat % 2)),
            lon + (k % 2) * (1 - 2 * (lon % 2)),
        )

    def load(n, src, dst):
        return pltpu.make_async_copy(src, dst, load_sem.at[n])

    loads = [
        load(0, maps_hbm, maps),
        load(1, w_qkv_fine_hbm, w_qkv_fine),
        load(2, bias_fine_hbm, bias_fine.at[0]),
        load(3, w_out_fine_hbm, w_out_fine),
        load(4, w_merge_hbm, w_merge),
        load(5, w_qkv_coarse_hbm, w_qkv_coarse),
        load(6, bias_coarse_hbm, bias_coarse),
    ]
    token_loads = [
        pltpu.make_async_copy(
            tokens_hbm.at[pl.ds(2 * c, 2)], tokens.at[c], token_sem.at[c]
        )
        for c in range(n_chunks)
    ]
    token_loads[0].start()
    loads[0].start()
    for copy in token_loads[1:]:
        copy.start()
    for copy in loads[1:]:
        copy.start()

    barrier = pltpu.get_barrier_semaphore()
    for near in (at(0, -1), at(0, 1), at(-1, 0), at(1, 0), at(-1, -1), at(1, 1), partner(3)):
        pl.semaphore_signal(barrier, inc=1, device_id=near, device_id_type=MESH)
    padded[...] = jnp.zeros_like(padded)
    pl.semaphore_wait(barrier, 7)
    loads[0].wait()

    def way(c):
        return 2 * (c % 2) - 1

    def quarter(c, k):
        return 3 - k + (c % 2) * (2 * k - 3)

    def fine_copy(c, k):
        q = quarter(c, k)
        return pltpu.make_async_remote_copy(
            fine_send.at[c, q],
            fine_recv.at[c, q],
            fine_ssem.at[c, k],
            fine_rsem.at[c, k],
            device_id=at(k // 2 * way(c), k % 2 * way(c)),
            device_id_type=MESH,
        )

    def heads_copy(c, k):
        q = quarter(c, k)
        return pltpu.make_async_remote_copy(
            heads_send.at[c, q],
            heads_recv.at[c, q],
            heads_ssem.at[c, k],
            heads_rsem.at[c, k],
            device_id=at(-(k // 2) * way(c), -(k % 2) * way(c)),
            device_id_type=MESH,
        )

    def other(k):
        mine_lat, mine_lon = lat % 2, lon % 2
        to_lat = mine_lat + (k // 2) * (1 - 2 * mine_lat)
        to_lon = mine_lon + (k % 2) * (1 - 2 * mine_lon)
        return to_lat * 2 + to_lon

    def coarse_copy(c, k):
        start = pl.multiple_of(other(k) * STEP, STEP)
        return pltpu.make_async_remote_copy(
            coarse_in.at[c, pl.ds(start, PIECE)],
            coarse_recv.at[c, member],
            coarse_ssem.at[c, k],
            coarse_rsem.at[c, k],
            device_id=partner(k),
            device_id_type=MESH,
        )

    def back_copy(c, k):
        return pltpu.make_async_remote_copy(
            back_send.at[c, other(k)],
            back_recv.at[c, member],
            back_ssem.at[c, k],
            back_rsem.at[c, k],
            device_id=partner(k),
            device_id_type=MESH,
        )

    def nat_rows(c, w):
        return padded[c, pl.ds(w * WLEV * ROWS, WLEV * ROWS)].reshape(NAT, D1)

    def quart_rows(ref, c, w, order):
        start = pl.multiple_of(w * STEP, STEP)
        return jnp.concatenate([ref[c, q, pl.ds(start, PIECE)] for q in order], axis=0)

    def put_quarters(c, send, recv, order):
        for n, q in enumerate(order):
            send[c, q] = assemble(lambda w: pieces[w, pl.ds(n * PIECE, PIECE)])
        own = quarter(c, 0)
        recv[c, own] = send[c, own]

    def send_tokens(c, _):
        for n in range(n_chunks):

            @pl.when(c == n)
            def _():
                token_loads[n].wait()

        block = tokens[c].reshape(2 * 4 * ROWS, COLS, D1)
        padded[c, :, pl.ds(0, COLS)] = block

        def one(w, _):
            pieces[w] = dot(maps[TO_QUART, w], nat_rows(c, w)).astype(jnp.bfloat16)
            return 0

        lax.fori_loop(0, NW, one, 0)
        put_quarters(c, fine_send, fine_recv, IN_TILE)
        for k in range(1, 4):
            fine_copy(c, k).start()
        return 0

    lax.fori_loop(0, n_chunks, send_tokens, 0)

    loads[1].wait()
    loads[2].wait()
    token_q = lax.broadcasted_iota(jnp.int32, (WIN, WIN), 0)
    token_k = lax.broadcasted_iota(jnp.int32, (WIN, WIN), 1)
    late_q = (token_q % (ROWS * COLS)) >= HALF_R * COLS
    late_k = (token_k % (ROWS * COLS)) >= HALF_R * COLS
    mask = jnp.where(late_q == late_k, 0.0, NEG)
    for h in range(D1 // HS):
        bias_fine[1, h] = bias_fine[0, h] + mask
    loads[3].wait()
    loads[4].wait()
    loads[5].wait()
    loads[6].wait()

    def fine_attention(c):
        for k in range(1, 4):
            fine_copy(c, k).wait_recv()

        def gather(w, _):
            rows = dot(maps[TO_WIN, w][:WIN], quart_rows(fine_recv, c, w, IN_WINDOW))
            start = pl.multiple_of(w * WIN, 16)
            xn[pl.ds(start, WIN)] = normed(rows, gain_fine[...])
            return 0

        lax.fori_loop(0, NW, gather, 0)
        for n in range(3):
            part = dot(xn[...], w_qkv_fine[:, n * D1 : (n + 1) * D1])
            if n == 0:
                part = part.astype(jnp.bfloat16) * jnp.bfloat16(HS**-0.5)
            qkv[:, n * D1 : (n + 1) * D1] = part.astype(jnp.bfloat16)
        odd = c % 2
        at_edge = lat == (1 - odd) * (n_lat - 1)
        which = jnp.where(at_edge, 1, 0)

        def window(w, _):
            rows = pl.ds(pl.multiple_of(w * WIN, 16), WIN)
            heads = []
            for pair in range(D1 // 128):
                lanes = [pl.ds(n * D1 + pair * 128, 128) for n in range(3)]
                heads.append(
                    attend_pair(
                        qkv[rows, lanes[0]],
                        qkv[rows, lanes[1]],
                        qkv[rows, lanes[2]],
                        bias_fine[which, 2 * pair],
                        bias_fine[which, 2 * pair + 1],
                    )
                )
            heads = jnp.concatenate(heads, axis=1)
            pieces[w] = dot(maps[FROM_WIN, w][:, :WIN], heads).astype(jnp.bfloat16)
            return 0

        lax.fori_loop(0, NW, window, 0)
        put_quarters(c, heads_send, heads_recv, IN_WINDOW)
        for k in range(1, 4):
            heads_copy(c, k).start()

    def merge(c):
        for k in range(1, 4):
            heads_copy(c, k).wait_recv()

        def regroup(w, _):
            rows = quart_rows(heads_recv, c, w, IN_TILE)
            pieces[w] = dot(maps[HEADS_GROUP, w], rows).astype(jnp.bfloat16)
            start = pl.multiple_of(w * NAT, 16)
            heads_nat[c, pl.ds(start, NAT)] = dot(maps[HEADS_NAT, w], rows).astype(jnp.bfloat16)
            return 0

        lax.fori_loop(0, NW, regroup, 0)
        pltpu.make_async_copy(heads_nat.at[c], heads_nat_hbm.at[c], out_sem.at[0, c]).start()
        for g in range(4):
            rows = assemble(lambda w: pieces[w, pl.ds(g * PIECE, PIECE)])
            group_heads[pl.ds(g * CROWS, CROWS)] = rows

        def regroup_tokens(w, _):
            pieces[w] = dot(maps[TO_GROUP, w], nat_rows(c, w)).astype(jnp.bfloat16)
            return 0

        lax.fori_loop(0, NW, regroup_tokens, 0)
        fine_rows[...] = dot(group_heads[...], w_out_fine[...])
        total = jnp.zeros((CROWS, 1), jnp.float32)
        for g in range(4):
            rows = pl.ds(g * CROWS, CROWS)
            own = assemble(lambda w: pieces[w, pl.ds(g * PIECE, PIECE)])
            values = fine_rows[rows] + own.astype(jnp.float32)
            fine_rows[rows] = values
            total = total + jnp.sum(values, axis=-1, keepdims=True)
        average = total / (4 * D1)
        total = jnp.zeros((CROWS, 1), jnp.float32)
        for g in range(4):
            centred = fine_rows[pl.ds(g * CROWS, CROWS)] - average
            total = total + jnp.sum(centred * centred, axis=-1, keepdims=True)
        inverse = lax.rsqrt(total / (4 * D1) + EPS)
        merged = jnp.zeros((CROWS, D2), jnp.float32)
        for g in range(4):
            lanes = pl.ds(g * D1, D1)
            centred = fine_rows[pl.ds(g * CROWS, CROWS)] - average
            part = (centred * inverse * gain_merge[:, lanes]).astype(jnp.bfloat16)
            merged = merged + dot(part, w_merge[lanes])
        coarse_in[c] = merged.astype(jnp.bfloat16)
        start = pl.multiple_of(member * STEP, STEP)
        coarse_recv[c, member] = coarse_in[c, pl.ds(start, PIECE)]
        for k in range(1, 4):
            coarse_copy(c, k).start()
        pltpu.make_async_copy(coarse_in.at[c], coarse_in_hbm.at[c], out_sem.at[1, c]).start()

    def coarse_attention(c):
        for k in range(1, 4):
            coarse_copy(c, k).wait_recv()
        rows = jnp.concatenate([coarse_recv[c, m] for m in range(4)], axis=0)
        values = dot(maps[TO_WIN, member][:WIN], rows)
        xn_coarse[...] = normed(values, gain_coarse[...])
        for n in range(3):
            lanes = pl.ds(n * D2, D2)
            part = dot(xn_coarse[...], w_qkv_coarse[:, lanes]).astype(jnp.bfloat16)
            if n == 0:
                part = part * jnp.bfloat16(HS**-0.5)
            qkv_coarse[:, lanes] = part
        heads = []
        for pair in range(D2 // 128):
            lanes = [pl.ds(n * D2 + pair * 128, 128) for n in range(3)]
            heads.append(
                attend_pair(
                    qkv_coarse[:, lanes[0]],
                    qkv_coarse[:, lanes[1]],
                    qkv_coarse[:, lanes[2]],
                    bias_coarse[2 * pair],
                    bias_coarse[2 * pair + 1],
                )
            )
        heads = jnp.concatenate(heads, axis=1)
        rows = dot(maps[FROM_WIN, member][:, :WIN], heads).astype(jnp.bfloat16)
        for m in range(4):
            back_send[c, m] = rows[m * PIECE : (m + 1) * PIECE]
        back_recv[c, member] = back_send[c, member]
        for k in range(1, 4):
            back_copy(c, k).start()

    def finish(c):
        for k in range(1, 4):
            back_copy(c, k).wait_recv()
        heads_coarse[c] = assemble(lambda w: back_recv[c, w])
        pltpu.make_async_copy(heads_coarse.at[c], heads_coarse_hbm.at[c], out_sem.at[2, c]).start()

    def step(s, _):
        for depth, stage in enumerate((fine_attention, merge, coarse_attention, finish)):

            @pl.when((s >= depth) & (s < n_chunks + depth))
            def _():
                stage(s - depth)

        return 0

    lax.fori_loop(0, n_chunks + 3, step, 0)

    def drain(c, _):
        for k in range(1, 4):
            fine_copy(c, k).wait_send()
            heads_copy(c, k).wait_send()
            coarse_copy(c, k).wait_send()
            back_copy(c, k).wait_send()
        pltpu.make_async_copy(heads_nat.at[c], heads_nat_hbm.at[c], out_sem.at[0, c]).wait()
        pltpu.make_async_copy(coarse_in.at[c], coarse_in_hbm.at[c], out_sem.at[1, c]).wait()
        pltpu.make_async_copy(heads_coarse.at[c], heads_coarse_hbm.at[c], out_sem.at[2, c]).wait()
        return 0

    lax.fori_loop(0, n_chunks, drain, 0)


def last_kernel(
    tokens, heads_nat, coarse_in, heads_coarse, w_out_fine, w_out_coarse, spread, fine_out, coarse_out
):
    fine = dot(heads_nat[0], w_out_fine[...]).reshape(2, 4, ROWS, 16, D1)
    fine_out[...] = fine[:, :, :, :COLS] + tokens[...].astype(jnp.float32)
    wide = dot(spread[...], jnp.concatenate([heads_coarse[0], coarse_in[0]], axis=1))
    coarse = dot(wide[:, :D2].astype(jnp.bfloat16), w_out_coarse[...]) + wide[:, D2:]
    coarse_out[...] = coarse.reshape(2, 4, HALF_R, 8, D2)[:, :, :, :HALF_C]


def body(
    fine_tokens,
    gain_fine,
    w_qkv_fine,
    bias_fine,
    w_out_fine,
    gain_merge,
    w_merge,
    gain_coarse,
    w_qkv_coarse,
    bias_coarse,
    w_out_coarse,
):
    batch = fine_tokens.shape[0]
    chunks = batch // 2
    bf16, f32 = jnp.bfloat16, jnp.float32
    maps = jnp.asarray(row_maps(), bf16)
    spread = jnp.asarray(spread_map(), bf16)
    hbm = pl.BlockSpec(memory_space=pl.ANY)
    vmem = pl.BlockSpec(memory_space=pltpu.VMEM)
    dma = pltpu.SemaphoreType.DMA
    heads_nat, coarse_in, heads_coarse = pl.pallas_call(
        functools.partial(main_kernel, chunks, lax.axis_size("lat"), lax.axis_size("lon")),
        out_shape=(
            jax.ShapeDtypeStruct((chunks, NW * NAT, D1), bf16),
            jax.ShapeDtypeStruct((chunks, CROWS, D2), bf16),
            jax.ShapeDtypeStruct((chunks, CROWS, D2), bf16),
        ),
        in_specs=[hbm, vmem, hbm, hbm, hbm, vmem, hbm, vmem, hbm, hbm, hbm],
        out_specs=(hbm, hbm, hbm),
        scratch_shapes=[
            pltpu.VMEM((chunks, 2, 4, ROWS, COLS, D1), bf16),
            pltpu.VMEM(w_qkv_fine.shape, bf16),
            pltpu.VMEM((2,) + bias_fine.shape, f32),
            pltpu.VMEM(w_out_fine.shape, bf16),
            pltpu.VMEM(w_merge.shape, bf16),
            pltpu.VMEM(w_qkv_coarse.shape, bf16),
            pltpu.VMEM(bias_coarse.shape, f32),
            pltpu.VMEM(maps.shape, bf16),
            pltpu.VMEM((chunks, 2 * 4 * ROWS, 16, D1), bf16),
            pltpu.VMEM((NW, 4 * PIECE, D1), bf16),
            pltpu.VMEM((chunks, 4, CROWS, D1), bf16),
            pltpu.VMEM((chunks, 4, CROWS, D1), bf16),
            pltpu.VMEM((NW * WIN, D1), bf16),
            pltpu.VMEM((NW * WIN, 3 * D1), bf16),
            pltpu.VMEM((chunks, 4, CROWS, D1), bf16),
            pltpu.VMEM((chunks, 4, CROWS, D1), bf16),
            pltpu.VMEM((4 * CROWS, D1), bf16),
            pltpu.VMEM((4 * CROWS, D1), f32),
            pltpu.VMEM((chunks, NW * NAT, D1), bf16),
            pltpu.VMEM((chunks, CROWS, D2), bf16),
            pltpu.VMEM((chunks, 4, PIECE, D2), bf16),
            pltpu.VMEM((WIN, D2), bf16),
            pltpu.VMEM((WIN, 3 * D2), bf16),
            pltpu.VMEM((chunks, 4, PIECE, D2), bf16),
            pltpu.VMEM((chunks, 4, PIECE, D2), bf16),
            pltpu.VMEM((chunks, CROWS, D2), bf16),
            dma((7,)),
            dma((chunks,)),
        ]
        + [dma((chunks, 4)) for _ in range(8)]
        + [dma((3, chunks))],
        compiler_params=pltpu.CompilerParams(
            collective_id=0, has_side_effects=True, vmem_limit_bytes=VMEM_LIMIT
        ),
        name="window_levels",
    )(
        fine_tokens,
        gain_fine[None],
        w_qkv_fine,
        bias_fine,
        w_out_fine,
        gain_merge[None],
        w_merge,
        gain_coarse[None],
        w_qkv_coarse,
        bias_coarse,
        maps,
    )
    chunk3 = lambda c: (c, 0, 0)
    chunk5 = lambda c: (c, 0, 0, 0, 0)
    whole = lambda c: (0, 0)
    return pl.pallas_call(
        last_kernel,
        grid=(chunks,),
        out_shape=(
            jax.ShapeDtypeStruct(fine_tokens.shape, f32),
            jax.ShapeDtypeStruct((batch, 4, HALF_R, HALF_C, D2), f32),
        ),
        in_specs=[
            pl.BlockSpec((2, 4, ROWS, COLS, D1), chunk5),
            pl.BlockSpec((1, NW * NAT, D1), chunk3),
            pl.BlockSpec((1, CROWS, D2), chunk3),
            pl.BlockSpec((1, CROWS, D2), chunk3),
            pl.BlockSpec((D1, D1), whole),
            pl.BlockSpec((D2, D2), whole),
            pl.BlockSpec(spread.shape, whole),
        ],
        out_specs=(
            pl.BlockSpec((2, 4, ROWS, COLS, D1), chunk5),
            pl.BlockSpec((2, 4, HALF_R, HALF_C, D2), chunk5),
        ),
        compiler_params=pltpu.CompilerParams(vmem_limit_bytes=VMEM_LIMIT),
        name="last_projections",
    )(fine_tokens, heads_nat, coarse_in, heads_coarse, w_out_fine, w_out_coarse, spread)


def solution(mesh):
    tile = P(None, None, "lat", "lon", None)
    return jax.shard_map(
        body,
        mesh=mesh,
        in_specs=(tile,) + (P(),) * 10,
        out_specs=(tile, tile),
        check_vma=False,
    )
```

```python
import functools

import jax
import jax.numpy as jnp
import numpy as np
from jax import lax
from jax.experimental import pallas as pl
from jax.experimental.pallas import tpu as pltpu
from jax.sharding import PartitionSpec as P

EPS = 1e-05
NEG = -1e30
ROWS, COLS, LEVELS, WLEV, HS = 6, 12, 4, 2, 64
HALF_R, HALF_C = ROWS // 2, COLS // 2
WIN = WLEV * ROWS * COLS
PAIR = 2 * WIN
NW = 4
CROWS = 2 * HALF_R * HALF_C * LEVELS
D1, D2 = 512, 1024
TO_SEND, TO_WIN, FROM_WIN = range(3)
MESH = pl.DeviceIdType.MESH
VMEM_LIMIT = 58 * 1024 * 1024


def pair_maps():
    to_win = np.zeros((PAIR, PAIR), np.float32)
    for lev in range(LEVELS):
        for r in range(ROWS):
            for c in range(COLS):
                q = (1 - r // HALF_R) * 2 + 1 - c // HALF_C
                src = ((q * HALF_R + r % HALF_R) * HALF_C + c % HALF_C) * LEVELS + lev
                win = lev // WLEV * WIN + (lev % WLEV * ROWS + r) * COLS + c
                to_win[win, src] = 1
    return np.stack([to_win, to_win.T])


def coarse_maps():
    to_send = np.zeros((CROWS, CROWS), np.float32)
    to_win = np.zeros((CROWS, CROWS), np.float32)
    part = CROWS // NW
    for b in range(2):
        for r in range(HALF_R):
            for c in range(HALF_C):
                for lev in range(LEVELS):
                    nat = ((b * HALF_R + r) * HALF_C + c) * LEVELS + lev
                    t = (lev % WLEV * HALF_R + r) * HALF_C + c
                    to_send[(b * 2 + lev // WLEV) * part + t, nat] = 1
    for lev in range(WLEV):
        for r in range(ROWS):
            for c in range(COLS):
                m = r // HALF_R * 2 + c // HALF_C
                t = (lev * HALF_R + r % HALF_R) * HALF_C + c % HALF_C
                to_win[(lev * ROWS + r) * COLS + c, m * part + t] = 1
    return np.stack([to_send, to_win, to_win.T])


def dot(a, b):
    return jnp.dot(a, b, preferred_element_type=jnp.float32)


def dot_t(a, b):
    return lax.dot_general(a, b, (((1,), (1,)), ((), ())), preferred_element_type=jnp.float32)


def normed(values, gain):
    average = jnp.mean(values, axis=-1, keepdims=True)
    centred = values - average
    variance = jnp.mean(centred * centred, axis=-1, keepdims=True)
    return (centred * lax.rsqrt(variance + EPS) * gain).astype(jnp.bfloat16)


def attend_pair(query, key, value, bias0, bias1):
    low = lax.broadcasted_iota(jnp.int32, (WIN, 128), 1) < HS
    one = jnp.ones((), jnp.bfloat16)
    zero = jnp.zeros((), jnp.bfloat16)
    results = []
    for side, bias in ((low, bias0), (jnp.logical_not(low), bias1)):
        scores = dot_t(jnp.where(side, query, zero), key) + bias
        top = jnp.max(scores, axis=-1, keepdims=True)
        probs = jnp.exp(scores - top).astype(jnp.bfloat16)
        results.append(dot(probs, jnp.where(side, value, one)))
    total = jnp.where(low, results[0], results[1])
    weight = pltpu.roll(jnp.where(low, results[1], results[0]), HS, 1)
    return (total / weight).astype(jnp.bfloat16)


def main_kernel(
    n_chunks,
    n_lat,
    n_lon,
    tokens_hbm,
    gain_fine,
    w_qkv_fine_hbm,
    bias_fine_hbm,
    w_out_fine_hbm,
    gain_merge,
    w_merge_hbm,
    gain_coarse,
    w_qkv_coarse_hbm,
    bias_coarse_hbm,
    maps_hbm,
    coarse_maps_hbm,
    heads_hbm,
    coarse_in_hbm,
    heads_coarse_hbm,
    tokens,
    w_qkv_fine,
    bias_fine,
    w_out_fine,
    w_merge,
    w_qkv_coarse,
    bias_coarse,
    maps,
    cmaps,
    fine_recv,
    xn,
    qkv,
    win_heads,
    heads_send,
    heads,
    fine_rows,
    merged,
    coarse_in,
    coarse_send,
    coarse_recv,
    xn_coarse,
    qkv_coarse,
    back_send,
    back_recv,
    load_sem,
    token_sem,
    own_sem,
    fine_ssem,
    fine_rsem,
    heads_ssem,
    heads_rsem,
    coarse_ssem,
    coarse_rsem,
    back_ssem,
    back_rsem,
    out_sem,
):
    lat = lax.axis_index("lat")
    lon = lax.axis_index("lon")
    member = (lat % 2) * 2 + lon % 2

    def at(dlat, dlon):
        return (lax.rem(lat + dlat + n_lat, n_lat), lax.rem(lon + dlon + n_lon, n_lon))

    def partner(k):
        return (
            lat + (k // 2) * (1 - 2 * (lat % 2)),
            lon + (k % 2) * (1 - 2 * (lon % 2)),
        )

    def way(c):
        return 2 * (c % 2) - 1

    def quarter(c, k):
        return 3 - k + (c % 2) * (2 * k - 3)

    def tile_part(ref, c, q):
        return ref.at[
            pl.ds(2 * c, 2), pl.ds(q // 2 * HALF_R, HALF_R), pl.ds(q % 2 * HALF_C, HALF_C)
        ]

    def fine_copy(c, k):
        q = quarter(c, k)
        return pltpu.make_async_remote_copy(
            tile_part(tokens_hbm, c, q),
            fine_recv.at[c, q],
            fine_ssem.at[c, k],
            fine_rsem.at[c, k],
            device_id=at(k // 2 * way(c), k % 2 * way(c)),
            device_id_type=MESH,
        )

    def own_copy(c):
        q = quarter(c, 0)
        return pltpu.make_async_copy(
            tile_part(tokens_hbm, c, q), fine_recv.at[c, q], own_sem.at[c]
        )

    def heads_copy(c, k):
        q = quarter(c, k)
        return pltpu.make_async_remote_copy(
            heads_send.at[c, q],
            tile_part(heads, c, q),
            heads_ssem.at[c, k],
            heads_rsem.at[c, k],
            device_id=at(-(k // 2) * way(c), -(k % 2) * way(c)),
            device_id_type=MESH,
        )

    def other(k):
        mine_lat, mine_lon = lat % 2, lon % 2
        to_lat = mine_lat + (k // 2) * (1 - 2 * mine_lat)
        to_lon = mine_lon + (k % 2) * (1 - 2 * mine_lon)
        return to_lat * 2 + to_lon

    def group_copy(c, k, send, recv, ssem, rsem):
        return pltpu.make_async_remote_copy(
            send.at[c, other(k)],
            recv.at[c, member],
            ssem.at[c, k],
            rsem.at[c, k],
            device_id=partner(k),
            device_id_type=MESH,
        )

    def coarse_copy(c, k):
        return group_copy(c, k, coarse_send, coarse_recv, coarse_ssem, coarse_rsem)

    def back_copy(c, k):
        return group_copy(c, k, back_send, back_recv, back_ssem, back_rsem)

    def token_copy(c):
        part = pl.ds(2 * c, 2)
        return pltpu.make_async_copy(tokens_hbm.at[part], tokens.at[part], token_sem.at[c])

    def result_copy(n, c):
        part = pl.ds(2 * c, 2)
        src, dst = (
            (heads.at[part], heads_hbm.at[part]),
            (coarse_in.at[c], coarse_in_hbm.at[c]),
            (back_recv.at[c], heads_coarse_hbm.at[c]),
        )[n]
        return pltpu.make_async_copy(src, dst, out_sem.at[n, c])

    def load(n, src, dst):
        return pltpu.make_async_copy(src, dst, load_sem.at[n])

    loads = [
        load(0, maps_hbm, maps),
        load(1, w_qkv_fine_hbm, w_qkv_fine),
        load(2, bias_fine_hbm, bias_fine.at[0]),
        load(3, w_out_fine_hbm, w_out_fine),
        load(4, w_merge_hbm, w_merge),
        load(5, coarse_maps_hbm, cmaps),
        load(6, w_qkv_coarse_hbm, w_qkv_coarse),
        load(7, bias_coarse_hbm, bias_coarse),
    ]

    barrier = pltpu.get_barrier_semaphore()
    for near in (at(0, -1), at(0, 1), at(-1, 0), at(1, 0), at(-1, -1), at(1, 1), partner(3)):
        pl.semaphore_signal(barrier, inc=1, device_id=near, device_id_type=MESH)
    pl.semaphore_wait(barrier, 7)

    def send_tokens(c, _):
        for k in (3, 2, 1):
            fine_copy(c, k).start()
        own_copy(c).start()
        return 0

    lax.fori_loop(0, n_chunks, send_tokens, 0)
    for copy in loads[:3]:
        copy.start()
    for c in range(n_chunks):
        token_copy(c).start()
    for copy in loads[3:]:
        copy.start()

    loads[2].wait()
    token_q = lax.broadcasted_iota(jnp.int32, (WIN, WIN), 0)
    token_k = lax.broadcasted_iota(jnp.int32, (WIN, WIN), 1)
    late_q = (token_q % (ROWS * COLS)) >= HALF_R * COLS
    late_k = (token_k % (ROWS * COLS)) >= HALF_R * COLS
    mask = jnp.where(late_q == late_k, 0.0, NEG)
    for h in range(D1 // HS):
        bias_fine[1, h] = bias_fine[0, h] + mask
    loads[0].wait()
    loads[1].wait()

    def fine_attention(c):
        own_copy(c).wait()
        for k in (1, 2, 3):
            fine_copy(c, k).wait_recv()
        for b in range(2):
            rows = fine_recv[c, :, b].reshape(PAIR, D1)
            xn[pl.ds(b * PAIR, PAIR)] = normed(dot(maps[0], rows), gain_fine[...])
        for n in range(3):
            part = dot(xn[...], w_qkv_fine[:, n * D1 : (n + 1) * D1]).astype(jnp.bfloat16)
            if n == 0:
                part = part * jnp.bfloat16(HS**-0.5)
            qkv[:, n * D1 : (n + 1) * D1] = part
        at_edge = lat == (1 - c % 2) * (n_lat - 1)
        which = jnp.where(at_edge, 1, 0)

        def window(w, _):
            rows = pl.ds(pl.multiple_of(w * WIN, 16), WIN)
            for pair in range(D1 // 128):
                lanes = [pl.ds(n * D1 + pair * 128, 128) for n in range(3)]
                win_heads[rows, lanes[0]] = attend_pair(
                    qkv[rows, lanes[0]],
                    qkv[rows, lanes[1]],
                    qkv[rows, lanes[2]],
                    bias_fine[which, 2 * pair],
                    bias_fine[which, 2 * pair + 1],
                )
            return 0

        lax.fori_loop(0, NW, window, 0)
        for b in range(2):
            rows = dot(maps[1], win_heads[pl.ds(b * PAIR, PAIR)]).astype(jnp.bfloat16)
            heads_send[c, :, b] = rows.reshape(4, HALF_R, HALF_C, LEVELS, D1)
        for k in (3, 2, 1):
            heads_copy(c, k).start()
        own = quarter(c, 0)
        tile_part(heads, c, own)[...] = heads_send[c, own]

    def merge(c):
        @pl.when(c == 0)
        def _():
            loads[3].wait()
            loads[4].wait()
            loads[5].wait()

        token_copy(c).wait()
        for k in (1, 2, 3):
            heads_copy(c, k).wait_recv()
        result_copy(0, c).start()
        part = pl.ds(2 * c, 2)
        rows = dot(heads[part].reshape(4 * CROWS, D1), w_out_fine[...])
        rows = rows + tokens[part].reshape(4 * CROWS, D1).astype(jnp.float32)
        fine_rows[...] = rows.reshape(2, HALF_R, 2, HALF_C, 2, LEVELS, D1)
        total = jnp.zeros((CROWS, 1), jnp.float32)
        for g in range(4):
            values = fine_rows[:, :, g % 2, :, g // 2].reshape(CROWS, D1)
            total = total + jnp.sum(values, axis=-1, keepdims=True)
        average = total / (4 * D1)
        total = jnp.zeros((CROWS, 1), jnp.float32)
        for g in range(4):
            centred = fine_rows[:, :, g % 2, :, g // 2].reshape(CROWS, D1) - average
            total = total + jnp.sum(centred * centred, axis=-1, keepdims=True)
        inverse = lax.rsqrt(total / (4 * D1) + EPS)
        for g in range(4):
            lanes = pl.ds(g * D1, D1)
            centred = fine_rows[:, :, g % 2, :, g // 2].reshape(CROWS, D1) - average
            merged[:, lanes] = (centred * inverse * gain_merge[:, lanes]).astype(jnp.bfloat16)
        coarse = dot(merged[...], w_merge[...]).astype(jnp.bfloat16)
        coarse_in[c] = coarse
        rows = dot(cmaps[TO_SEND], coarse).astype(jnp.bfloat16)
        coarse_send[c] = rows.reshape(coarse_send.shape[1:])
        for k in (3, 2, 1):
            coarse_copy(c, k).start()
        coarse_recv[c, member] = coarse_send[c, member]
        result_copy(1, c).start()

    def coarse_attention(c):
        @pl.when(c == 0)
        def _():
            loads[6].wait()
            loads[7].wait()

        for k in (1, 2, 3):
            coarse_copy(c, k).wait_recv()
        values = dot(cmaps[TO_WIN], coarse_recv[c].reshape(WIN, D2))
        xn_coarse[...] = normed(values, gain_coarse[...])
        for n in range(3):
            lanes = pl.ds(n * D2, D2)
            part = dot(xn_coarse[...], w_qkv_coarse[:, lanes]).astype(jnp.bfloat16)
            if n == 0:
                part = part * jnp.bfloat16(HS**-0.5)
            qkv_coarse[:, lanes] = part
        results = []
        for pair in range(D2 // 128):
            lanes = [pl.ds(n * D2 + pair * 128, 128) for n in range(3)]
            results.append(
                attend_pair(
                    qkv_coarse[:, lanes[0]],
                    qkv_coarse[:, lanes[1]],
                    qkv_coarse[:, lanes[2]],
                    bias_coarse[2 * pair],
                    bias_coarse[2 * pair + 1],
                )
            )
        rows = dot(cmaps[FROM_WIN], jnp.concatenate(results, axis=1)).astype(jnp.bfloat16)
        back_send[c] = rows.reshape(back_send.shape[1:])
        for k in (3, 2, 1):
            back_copy(c, k).start()
        back_recv[c, member] = back_send[c, member]

    def finish(c):
        for k in (1, 2, 3):
            back_copy(c, k).wait_recv()
        result_copy(2, c).start()

    def step(s, _):
        for depth, stage in enumerate((fine_attention, merge, coarse_attention, finish)):

            @pl.when((s >= depth) & (s < n_chunks + depth))
            def _():
                stage(s - depth)

        return 0

    lax.fori_loop(0, n_chunks + 3, step, 0)

    def drain(c, _):
        for k in (1, 2, 3):
            fine_copy(c, k).wait_send()
            heads_copy(c, k).wait_send()
            coarse_copy(c, k).wait_send()
            back_copy(c, k).wait_send()
        for n in range(3):
            result_copy(n, c).wait()
        return 0

    lax.fori_loop(0, n_chunks, drain, 0)


def last_kernel(
    tokens, heads, coarse_in, heads_coarse, w_out_fine, w_out_coarse, maps, fine_out, coarse_out
):
    fine = dot(heads[...].reshape(4 * CROWS, D1), w_out_fine[...])
    fine = fine + tokens[...].reshape(4 * CROWS, D1).astype(jnp.float32)
    fine_out[...] = fine.reshape(fine_out.shape)
    rows = dot(maps[...], heads_coarse[...].reshape(CROWS, D2)).astype(jnp.bfloat16)
    coarse = dot(rows, w_out_coarse[...]) + coarse_in[0].astype(jnp.float32)
    coarse_out[...] = coarse.reshape(coarse_out.shape)


def body(
    fine_tokens,
    gain_fine,
    w_qkv_fine,
    bias_fine,
    w_out_fine,
    gain_merge,
    w_merge,
    gain_coarse,
    w_qkv_coarse,
    bias_coarse,
    w_out_coarse,
):
    tokens = fine_tokens.transpose(0, 2, 3, 1, 4)
    batch = tokens.shape[0]
    chunks = batch // 2
    bf16, f32 = jnp.bfloat16, jnp.float32
    maps = jnp.asarray(pair_maps(), bf16)
    cmaps = jnp.asarray(coarse_maps(), bf16)
    cmap_back = jnp.asarray(coarse_maps()[TO_SEND].T, bf16)
    hbm = pl.BlockSpec(memory_space=pl.ANY)
    vmem = pl.BlockSpec(memory_space=pltpu.VMEM)
    dma = pltpu.SemaphoreType.DMA
    slots = (chunks, NW, CROWS // NW // 4, 4, D2)
    heads, coarse_in, heads_coarse = pl.pallas_call(
        functools.partial(main_kernel, chunks, lax.axis_size("lat"), lax.axis_size("lon")),
        out_shape=(
            jax.ShapeDtypeStruct(tokens.shape, bf16),
            jax.ShapeDtypeStruct((chunks, CROWS, D2), bf16),
            jax.ShapeDtypeStruct(slots, bf16),
        ),
        in_specs=[hbm, vmem, hbm, hbm, hbm, vmem, hbm, vmem, hbm, hbm, hbm, hbm],
        out_specs=(hbm, hbm, hbm),
        scratch_shapes=[
            pltpu.VMEM(tokens.shape, bf16),
            pltpu.VMEM(w_qkv_fine.shape, bf16),
            pltpu.VMEM((2,) + bias_fine.shape, f32),
            pltpu.VMEM(w_out_fine.shape, bf16),
            pltpu.VMEM(w_merge.shape, bf16),
            pltpu.VMEM(w_qkv_coarse.shape, bf16),
            pltpu.VMEM(bias_coarse.shape, f32),
            pltpu.VMEM(maps.shape, bf16),
            pltpu.VMEM(cmaps.shape, bf16),
            pltpu.VMEM((chunks, 4, 2, HALF_R, HALF_C, LEVELS, D1), bf16),
            pltpu.VMEM((NW * WIN, D1), bf16),
            pltpu.VMEM((NW * WIN, 3 * D1), bf16),
            pltpu.VMEM((NW * WIN, D1), bf16),
            pltpu.VMEM((chunks, 4, 2, HALF_R, HALF_C, LEVELS, D1), bf16),
            pltpu.VMEM(tokens.shape, bf16),
            pltpu.VMEM((2, HALF_R, 2, HALF_C, 2, LEVELS, D1), f32),
            pltpu.VMEM((CROWS, 4 * D1), bf16),
            pltpu.VMEM((chunks, CROWS, D2), bf16),
            pltpu.VMEM(slots, bf16),
            pltpu.VMEM(slots, bf16),
            pltpu.VMEM((WIN, D2), bf16),
            pltpu.VMEM((WIN, 3 * D2), bf16),
            pltpu.VMEM(slots, bf16),
            pltpu.VMEM(slots, bf16),
            dma((8,)),
            dma((chunks,)),
            dma((chunks,)),
        ]
        + [dma((chunks, 4)) for _ in range(8)]
        + [dma((3, chunks))],
        compiler_params=pltpu.CompilerParams(
            collective_id=0, has_side_effects=True, vmem_limit_bytes=VMEM_LIMIT
        ),
        name="window_levels",
    )(
        tokens,
        gain_fine[None],
        w_qkv_fine,
        bias_fine,
        w_out_fine,
        gain_merge[None],
        w_merge,
        gain_coarse[None],
        w_qkv_coarse,
        bias_coarse,
        maps,
        cmaps,
    )
    chunk3 = lambda c: (c, 0, 0)
    chunk5 = lambda c: (c, 0, 0, 0, 0)
    whole = lambda c: (0, 0)
    fine_out, coarse_out = pl.pallas_call(
        last_kernel,
        grid=(chunks,),
        out_shape=(
            jax.ShapeDtypeStruct(tokens.shape, f32),
            jax.ShapeDtypeStruct((batch, HALF_R, HALF_C, LEVELS, D2), f32),
        ),
        in_specs=[
            pl.BlockSpec((2, ROWS, COLS, LEVELS, D1), chunk5),
            pl.BlockSpec((2, ROWS, COLS, LEVELS, D1), chunk5),
            pl.BlockSpec((1, CROWS, D2), chunk3),
            pl.BlockSpec((1,) + slots[1:], chunk5),
            pl.BlockSpec((D1, D1), whole),
            pl.BlockSpec((D2, D2), whole),
            pl.BlockSpec(cmap_back.shape, whole),
        ],
        out_specs=(
            pl.BlockSpec((2, ROWS, COLS, LEVELS, D1), chunk5),
            pl.BlockSpec((2, HALF_R, HALF_C, LEVELS, D2), chunk5),
        ),
        compiler_params=pltpu.CompilerParams(vmem_limit_bytes=VMEM_LIMIT),
        name="last_projections",
    )(tokens, heads, coarse_in, heads_coarse, w_out_fine, w_out_coarse, cmap_back)
    return fine_out.transpose(0, 3, 1, 2, 4), coarse_out.transpose(0, 3, 1, 2, 4)


def solution(mesh):
    tile = P(None, None, "lat", "lon", None)
    return jax.shard_map(
        body,
        mesh=mesh,
        in_specs=(tile,) + (P(),) * 10,
        out_specs=(tile, tile),
        check_vma=False,
    )
```

```python
import functools

import jax
import jax.numpy as jnp
import numpy as np
from jax import lax
from jax.experimental import pallas as pl
from jax.experimental.pallas import tpu as pltpu
from jax.sharding import PartitionSpec as P

EPS = 1e-05
NEG = -1e30
ROWS, COLS, LEVELS, WLEV, HS = 6, 12, 4, 2, 64
HALF_R, HALF_C = ROWS // 2, COLS // 2
WIN = WLEV * ROWS * COLS
PAIR = 2 * WIN
NW = 4
AHEAD = 2
CROWS = 2 * HALF_R * HALF_C * LEVELS
D1, D2 = 512, 1024
TO_SEND, TO_WIN, FROM_WIN, FROM_SEND = range(4)
MESH = pl.DeviceIdType.MESH
VMEM_LIMIT = 52 * 1024 * 1024


def pair_maps():
    to_win = np.zeros((PAIR, PAIR), np.float32)
    for lev in range(LEVELS):
        for r in range(ROWS):
            for c in range(COLS):
                q = (1 - r // HALF_R) * 2 + 1 - c // HALF_C
                src = ((q * HALF_R + r % HALF_R) * HALF_C + c % HALF_C) * LEVELS + lev
                win = lev // WLEV * WIN + (lev % WLEV * ROWS + r) * COLS + c
                to_win[win, src] = 1
    return np.stack([to_win, to_win.T])


def coarse_maps():
    to_send = np.zeros((CROWS, CROWS), np.float32)
    to_win = np.zeros((CROWS, CROWS), np.float32)
    part = CROWS // NW
    for b in range(2):
        for r in range(HALF_R):
            for c in range(HALF_C):
                for lev in range(LEVELS):
                    nat = ((b * HALF_R + r) * HALF_C + c) * LEVELS + lev
                    t = (lev % WLEV * HALF_R + r) * HALF_C + c
                    to_send[(b * 2 + lev // WLEV) * part + t, nat] = 1
    for lev in range(WLEV):
        for r in range(ROWS):
            for c in range(COLS):
                m = r // HALF_R * 2 + c // HALF_C
                t = (lev * HALF_R + r % HALF_R) * HALF_C + c % HALF_C
                to_win[(lev * ROWS + r) * COLS + c, m * part + t] = 1
    return np.stack([to_send, to_win, to_win.T, to_send.T])


def dot(a, b):
    return jnp.dot(a, b, preferred_element_type=jnp.float32)


def dot_t(a, b):
    return lax.dot_general(a, b, (((1,), (1,)), ((), ())), preferred_element_type=jnp.float32)


def normed(values, gain):
    average = jnp.mean(values, axis=-1, keepdims=True)
    centred = values - average
    variance = jnp.mean(centred * centred, axis=-1, keepdims=True)
    return (centred * lax.rsqrt(variance + EPS) * gain).astype(jnp.bfloat16)


def attend_pair(query, key, value, bias0, bias1):
    low = lax.broadcasted_iota(jnp.int32, (WIN, 128), 1) < HS
    one = jnp.ones((), jnp.bfloat16)
    zero = jnp.zeros((), jnp.bfloat16)
    results = []
    for side, bias in ((low, bias0), (jnp.logical_not(low), bias1)):
        scores = dot_t(jnp.where(side, query, zero), key) + bias
        top = jnp.max(scores, axis=-1, keepdims=True)
        probs = jnp.exp(scores - top).astype(jnp.bfloat16)
        results.append(dot(probs, jnp.where(side, value, one)))
    total = jnp.where(low, results[0], results[1])
    weight = pltpu.roll(jnp.where(low, results[1], results[0]), HS, 1)
    return (total / weight).astype(jnp.bfloat16)


def main_kernel(
    n_chunks,
    n_lat,
    n_lon,
    tokens_hbm,
    gain_fine,
    w_qkv_fine_hbm,
    bias_fine_hbm,
    w_out_fine_hbm,
    gain_merge,
    w_merge_hbm,
    gain_coarse,
    w_qkv_coarse_hbm,
    bias_coarse_hbm,
    maps_hbm,
    coarse_maps_hbm,
    w_out_coarse_hbm,
    fine_out,
    coarse_out,
    tokens,
    w_qkv_fine,
    bias_fine,
    w_out_fine,
    w_merge,
    w_qkv_coarse,
    bias_coarse,
    w_out_coarse,
    maps,
    cmaps,
    fine_recv,
    xn,
    qkv,
    win_heads,
    heads_send,
    heads,
    merged,
    coarse_in,
    coarse_send,
    coarse_recv,
    xn_coarse,
    qkv_coarse,
    back_send,
    back_recv,
    load_sem,
    token_sem,
    own_sem,
    fine_ssem,
    fine_rsem,
    heads_ssem,
    heads_rsem,
    coarse_ssem,
    coarse_rsem,
    back_ssem,
    back_rsem,
):
    lat = lax.axis_index("lat")
    lon = lax.axis_index("lon")
    member = (lat % 2) * 2 + lon % 2

    def at(dlat, dlon):
        return (lax.rem(lat + dlat + n_lat, n_lat), lax.rem(lon + dlon + n_lon, n_lon))

    def partner(k):
        return (
            lat + (k // 2) * (1 - 2 * (lat % 2)),
            lon + (k % 2) * (1 - 2 * (lon % 2)),
        )

    def way(c):
        return 2 * (c % 2) - 1

    def quarter(c, k):
        return 3 - k + (c % 2) * (2 * k - 3)

    def tile_part(ref, c, q):
        return ref.at[
            pl.ds(2 * c, 2), pl.ds(q // 2 * HALF_R, HALF_R), pl.ds(q % 2 * HALF_C, HALF_C)
        ]

    def fine_copy(c, k):
        q = quarter(c, k)
        return pltpu.make_async_remote_copy(
            tile_part(tokens_hbm, c, q),
            fine_recv.at[c, q],
            fine_ssem.at[c, k],
            fine_rsem.at[c, k],
            device_id=at(k // 2 * way(c), k % 2 * way(c)),
            device_id_type=MESH,
        )

    def own_copy(c):
        q = quarter(c, 0)
        return pltpu.make_async_copy(
            tile_part(tokens_hbm, c, q), fine_recv.at[c, q], own_sem.at[c]
        )

    def heads_copy(c, k):
        q = quarter(c, k)
        return pltpu.make_async_remote_copy(
            heads_send.at[c, q],
            tile_part(heads, c, q),
            heads_ssem.at[c, k],
            heads_rsem.at[c, k],
            device_id=at(-(k // 2) * way(c), -(k % 2) * way(c)),
            device_id_type=MESH,
        )

    def other(k):
        mine_lat, mine_lon = lat % 2, lon % 2
        to_lat = mine_lat + (k // 2) * (1 - 2 * mine_lat)
        to_lon = mine_lon + (k % 2) * (1 - 2 * mine_lon)
        return to_lat * 2 + to_lon

    def group_copy(c, k, send, recv, ssem, rsem):
        return pltpu.make_async_remote_copy(
            send.at[c, other(k)],
            recv.at[c, member],
            ssem.at[c, k],
            rsem.at[c, k],
            device_id=partner(k),
            device_id_type=MESH,
        )

    def coarse_copy(c, k):
        return group_copy(c, k, coarse_send, coarse_recv, coarse_ssem, coarse_rsem)

    def back_copy(c, k):
        return group_copy(c, k, back_send, back_recv, back_ssem, back_rsem)

    def token_copy(c):
        part = pl.ds(2 * c, 2)
        return pltpu.make_async_copy(tokens_hbm.at[part], tokens.at[part], token_sem.at[c])

    def load(n, src, dst):
        return pltpu.make_async_copy(src, dst, load_sem.at[n])

    loads = [
        load(0, maps_hbm, maps),
        load(1, w_qkv_fine_hbm, w_qkv_fine),
        load(2, bias_fine_hbm, bias_fine.at[0]),
        load(3, w_out_fine_hbm, w_out_fine),
        load(4, w_merge_hbm, w_merge),
        load(5, coarse_maps_hbm, cmaps),
        load(6, w_qkv_coarse_hbm, w_qkv_coarse),
        load(7, bias_coarse_hbm, bias_coarse),
        load(8, w_out_coarse_hbm, w_out_coarse),
    ]

    barrier = pltpu.get_barrier_semaphore()
    for near in (at(0, -1), at(0, 1), at(-1, 0), at(1, 0), at(-1, -1), at(1, 1), partner(3)):
        pl.semaphore_signal(barrier, inc=1, device_id=near, device_id_type=MESH)
    pl.semaphore_wait(barrier, 7)

    def send_tokens(c, _):
        for k in (3, 2, 1):
            fine_copy(c, k).start()
        own_copy(c).start()
        return 0

    lax.fori_loop(0, AHEAD, send_tokens, 0)
    for copy in loads[:3]:
        copy.start()
    for c in range(n_chunks):
        token_copy(c).start()
    for copy in loads[3:]:
        copy.start()

    loads[2].wait()
    token_q = lax.broadcasted_iota(jnp.int32, (WIN, WIN), 0)
    token_k = lax.broadcasted_iota(jnp.int32, (WIN, WIN), 1)
    late_q = (token_q % (ROWS * COLS)) >= HALF_R * COLS
    late_k = (token_k % (ROWS * COLS)) >= HALF_R * COLS
    mask = jnp.where(late_q == late_k, 0.0, NEG)
    for h in range(D1 // HS):
        bias_fine[1, h] = bias_fine[0, h] + mask
    loads[0].wait()
    loads[1].wait()

    def fine_attention(c):
        own_copy(c).wait()
        for k in (1, 2, 3):
            fine_copy(c, k).wait_recv()

        @pl.when(c + AHEAD < n_chunks)
        def _():
            send_tokens(c + AHEAD, 0)

        for b in range(2):
            rows = fine_recv[c, :, b].reshape(PAIR, D1)
            xn[pl.ds(b * PAIR, PAIR)] = normed(dot(maps[0], rows), gain_fine[...])
        for n in range(3):
            part = dot(xn[...], w_qkv_fine[:, n * D1 : (n + 1) * D1]).astype(jnp.bfloat16)
            if n == 0:
                part = part * jnp.bfloat16(HS**-0.5)
            qkv[:, n * D1 : (n + 1) * D1] = part
        at_edge = lat == (1 - c % 2) * (n_lat - 1)
        which = jnp.where(at_edge, 1, 0)

        def window(w, _):
            rows = pl.ds(pl.multiple_of(w * WIN, 16), WIN)
            for pair in range(D1 // 128):
                lanes = [pl.ds(n * D1 + pair * 128, 128) for n in range(3)]
                win_heads[rows, lanes[0]] = attend_pair(
                    qkv[rows, lanes[0]],
                    qkv[rows, lanes[1]],
                    qkv[rows, lanes[2]],
                    bias_fine[which, 2 * pair],
                    bias_fine[which, 2 * pair + 1],
                )
            return 0

        lax.fori_loop(0, NW, window, 0)
        for b in range(2):
            rows = dot(maps[1], win_heads[pl.ds(b * PAIR, PAIR)]).astype(jnp.bfloat16)
            heads_send[c, :, b] = rows.reshape(4, HALF_R, HALF_C, LEVELS, D1)
        for k in (3, 2, 1):
            heads_copy(c, k).start()
        own = quarter(c, 0)
        tile_part(heads, c, own)[...] = heads_send[c, own]

    def merge(c):
        @pl.when(c == 0)
        def _():
            loads[3].wait()
            loads[4].wait()
            loads[5].wait()

        token_copy(c).wait()
        for k in (1, 2, 3):
            heads_copy(c, k).wait_recv()
        part = pl.ds(2 * c, 2)
        rows = dot(heads[part].reshape(4 * CROWS, D1), w_out_fine[...])
        rows = rows + tokens[part].reshape(4 * CROWS, D1).astype(jnp.float32)
        fine_out[part] = rows.reshape(2, HALF_R, 2, HALF_C, 2, LEVELS, D1)
        total = jnp.zeros((CROWS, 1), jnp.float32)
        for g in range(4):
            values = fine_out[part, :, g % 2, :, g // 2].reshape(CROWS, D1)
            total = total + jnp.sum(values, axis=-1, keepdims=True)
        average = total / (4 * D1)
        total = jnp.zeros((CROWS, 1), jnp.float32)
        for g in range(4):
            centred = fine_out[part, :, g % 2, :, g // 2].reshape(CROWS, D1) - average
            total = total + jnp.sum(centred * centred, axis=-1, keepdims=True)
        inverse = lax.rsqrt(total / (4 * D1) + EPS)
        for g in range(4):
            lanes = pl.ds(g * D1, D1)
            centred = fine_out[part, :, g % 2, :, g // 2].reshape(CROWS, D1) - average
            merged[:, lanes] = (centred * inverse * gain_merge[:, lanes]).astype(jnp.bfloat16)
        coarse = dot(merged[...], w_merge[...]).astype(jnp.bfloat16)
        coarse_in[c] = coarse
        rows = dot(cmaps[TO_SEND], coarse).astype(jnp.bfloat16)
        coarse_send[c] = rows.reshape(coarse_send.shape[1:])
        for k in (3, 2, 1):
            coarse_copy(c, k).start()
        coarse_recv[c, member] = coarse_send[c, member]

    def coarse_attention(c):
        @pl.when(c == 0)
        def _():
            loads[6].wait()
            loads[7].wait()

        for k in (1, 2, 3):
            coarse_copy(c, k).wait_recv()
        values = dot(cmaps[TO_WIN], coarse_recv[c].reshape(WIN, D2))
        xn_coarse[...] = normed(values, gain_coarse[...])
        for n in range(3):
            lanes = pl.ds(n * D2, D2)
            part = dot(xn_coarse[...], w_qkv_coarse[:, lanes]).astype(jnp.bfloat16)
            if n == 0:
                part = part * jnp.bfloat16(HS**-0.5)
            qkv_coarse[:, lanes] = part
        results = []
        for pair in range(D2 // 128):
            lanes = [pl.ds(n * D2 + pair * 128, 128) for n in range(3)]
            results.append(
                attend_pair(
                    qkv_coarse[:, lanes[0]],
                    qkv_coarse[:, lanes[1]],
                    qkv_coarse[:, lanes[2]],
                    bias_coarse[2 * pair],
                    bias_coarse[2 * pair + 1],
                )
            )
        rows = dot(cmaps[FROM_WIN], jnp.concatenate(results, axis=1)).astype(jnp.bfloat16)
        back_send[c] = rows.reshape(back_send.shape[1:])
        for k in (3, 2, 1):
            back_copy(c, k).start()
        back_recv[c, member] = back_send[c, member]

    def finish(c):
        @pl.when(c == 0)
        def _():
            loads[8].wait()

        for k in (1, 2, 3):
            back_copy(c, k).wait_recv()
        rows = dot(cmaps[FROM_SEND], back_recv[c].reshape(CROWS, D2)).astype(jnp.bfloat16)
        rows = dot(rows, w_out_coarse[...]) + coarse_in[c].astype(jnp.float32)
        coarse_out[pl.ds(2 * c, 2)] = rows.reshape(2, HALF_R, HALF_C, LEVELS, D2)

    def step(s, _):
        for depth, stage in enumerate((fine_attention, merge, coarse_attention, finish)):

            @pl.when((s >= depth) & (s < n_chunks + depth))
            def _():
                stage(s - depth)

        return 0

    lax.fori_loop(0, n_chunks + 3, step, 0)

    def drain(c, _):
        for k in (1, 2, 3):
            fine_copy(c, k).wait_send()
            heads_copy(c, k).wait_send()
            coarse_copy(c, k).wait_send()
            back_copy(c, k).wait_send()
        return 0

    lax.fori_loop(0, n_chunks, drain, 0)


def body(
    fine_tokens,
    gain_fine,
    w_qkv_fine,
    bias_fine,
    w_out_fine,
    gain_merge,
    w_merge,
    gain_coarse,
    w_qkv_coarse,
    bias_coarse,
    w_out_coarse,
):
    tokens = fine_tokens.transpose(0, 2, 3, 1, 4)
    batch = tokens.shape[0]
    chunks = batch // 2
    bf16, f32 = jnp.bfloat16, jnp.float32
    maps = jnp.asarray(pair_maps(), bf16)
    cmaps = jnp.asarray(coarse_maps(), bf16)
    hbm = pl.BlockSpec(memory_space=pl.ANY)
    vmem = pl.BlockSpec(memory_space=pltpu.VMEM)
    dma = pltpu.SemaphoreType.DMA
    slots = (chunks, NW, CROWS // NW // 4, 4, D2)
    fine_out, coarse_out = pl.pallas_call(
        functools.partial(main_kernel, chunks, lax.axis_size("lat"), lax.axis_size("lon")),
        out_shape=(
            pltpu.VMEM((batch, HALF_R, 2, HALF_C, 2, LEVELS, D1), f32),
            pltpu.VMEM((batch, HALF_R, HALF_C, LEVELS, D2), f32),
        ),
        in_specs=[hbm, vmem, hbm, hbm, hbm, vmem, hbm, vmem, hbm, hbm, hbm, hbm, hbm],
        out_specs=(vmem, vmem),
        scratch_shapes=[
            pltpu.VMEM(tokens.shape, bf16),
            pltpu.VMEM(w_qkv_fine.shape, bf16),
            pltpu.VMEM((2,) + bias_fine.shape, f32),
            pltpu.VMEM(w_out_fine.shape, bf16),
            pltpu.VMEM(w_merge.shape, bf16),
            pltpu.VMEM(w_qkv_coarse.shape, bf16),
            pltpu.VMEM(bias_coarse.shape, f32),
            pltpu.VMEM(w_out_coarse.shape, bf16),
            pltpu.VMEM(maps.shape, bf16),
            pltpu.VMEM(cmaps.shape, bf16),
            pltpu.VMEM((chunks, 4, 2, HALF_R, HALF_C, LEVELS, D1), bf16),
            pltpu.VMEM((NW * WIN, D1), bf16),
            pltpu.VMEM((NW * WIN, 3 * D1), bf16),
            pltpu.VMEM((NW * WIN, D1), bf16),
            pltpu.VMEM((chunks, 4, 2, HALF_R, HALF_C, LEVELS, D1), bf16),
            pltpu.VMEM(tokens.shape, bf16),
            pltpu.VMEM((CROWS, 4 * D1), bf16),
            pltpu.VMEM((chunks, CROWS, D2), bf16),
            pltpu.VMEM(slots, bf16),
            pltpu.VMEM(slots, bf16),
            pltpu.VMEM((WIN, D2), bf16),
            pltpu.VMEM((WIN, 3 * D2), bf16),
            pltpu.VMEM(slots, bf16),
            pltpu.VMEM(slots, bf16),
            dma((9,)),
            dma((chunks,)),
            dma((chunks,)),
        ]
        + [dma((chunks, 4)) for _ in range(8)],
        compiler_params=pltpu.CompilerParams(
            collective_id=0, has_side_effects=True, vmem_limit_bytes=VMEM_LIMIT
        ),
        name="window_levels",
    )(
        tokens,
        gain_fine[None],
        w_qkv_fine,
        bias_fine,
        w_out_fine,
        gain_merge[None],
        w_merge,
        gain_coarse[None],
        w_qkv_coarse,
        bias_coarse,
        maps,
        cmaps,
        w_out_coarse,
    )
    fine_out = fine_out.reshape(tokens.shape)
    return fine_out.transpose(0, 3, 1, 2, 4), coarse_out.transpose(0, 3, 1, 2, 4)


def solution(mesh):
    tile = P(None, None, "lat", "lon", None)
    return jax.shard_map(
        body,
        mesh=mesh,
        in_specs=(tile,) + (P(),) * 10,
        out_specs=(tile, tile),
        check_vma=False,
    )
```

```python
import functools

import jax
import jax.numpy as jnp
import numpy as np
from jax import lax
from jax.experimental import pallas as pl
from jax.experimental.pallas import tpu as pltpu
from jax.sharding import PartitionSpec as P

EPS = 1e-05
NEG = -1e30
ROWS, COLS, LEVELS, WLEV, HS = 6, 12, 4, 2, 64
HALF_R, HALF_C = ROWS // 2, COLS // 2
WIN = WLEV * ROWS * COLS
PAIR = 2 * WIN
NW = 4
BEHIND = (0, 2, 4, 5)
AHEAD = 2
CROWS = 2 * HALF_R * HALF_C * LEVELS
D1, D2 = 512, 1024
TO_SEND, TO_WIN, FROM_WIN, FROM_SEND = range(4)
MESH = pl.DeviceIdType.MESH
VMEM_LIMIT = 52 * 1024 * 1024


def pair_maps():
    to_win = np.zeros((PAIR, PAIR), np.float32)
    for lev in range(LEVELS):
        for r in range(ROWS):
            for c in range(COLS):
                q = (1 - r // HALF_R) * 2 + 1 - c // HALF_C
                src = ((q * HALF_R + r % HALF_R) * HALF_C + c % HALF_C) * LEVELS + lev
                win = lev // WLEV * WIN + (lev % WLEV * ROWS + r) * COLS + c
                to_win[win, src] = 1
    return np.stack([to_win, to_win.T])


def coarse_maps():
    to_send = np.zeros((CROWS, CROWS), np.float32)
    to_win = np.zeros((CROWS, CROWS), np.float32)
    part = CROWS // NW
    for b in range(2):
        for r in range(HALF_R):
            for c in range(HALF_C):
                for lev in range(LEVELS):
                    nat = ((b * HALF_R + r) * HALF_C + c) * LEVELS + lev
                    t = (lev % WLEV * HALF_R + r) * HALF_C + c
                    to_send[(b * 2 + lev // WLEV) * part + t, nat] = 1
    for lev in range(WLEV):
        for r in range(ROWS):
            for c in range(COLS):
                m = r // HALF_R * 2 + c // HALF_C
                t = (lev * HALF_R + r % HALF_R) * HALF_C + c % HALF_C
                to_win[(lev * ROWS + r) * COLS + c, m * part + t] = 1
    return np.stack([to_send, to_win, to_win.T, to_send.T])


def dot(a, b):
    return jnp.dot(a, b, preferred_element_type=jnp.float32)


def dot_t(a, b):
    return lax.dot_general(a, b, (((1,), (1,)), ((), ())), preferred_element_type=jnp.float32)


def normed(values, gain):
    average = jnp.mean(values, axis=-1, keepdims=True)
    centred = values - average
    variance = jnp.mean(centred * centred, axis=-1, keepdims=True)
    return (centred * lax.rsqrt(variance + EPS) * gain).astype(jnp.bfloat16)


def attend_pair(query, key, value, bias0, bias1):
    low = lax.broadcasted_iota(jnp.int32, (WIN, 128), 1) < HS
    one = jnp.ones((), jnp.bfloat16)
    zero = jnp.zeros((), jnp.bfloat16)
    results = []
    for side, bias in ((low, bias0), (jnp.logical_not(low), bias1)):
        scores = dot_t(jnp.where(side, query, zero), key) + bias
        top = jnp.max(scores, axis=-1, keepdims=True)
        probs = jnp.exp(scores - top).astype(jnp.bfloat16)
        results.append(dot(probs, jnp.where(side, value, one)))
    total = jnp.where(low, results[0], results[1])
    weight = pltpu.roll(jnp.where(low, results[1], results[0]), HS, 1)
    return (total / weight).astype(jnp.bfloat16)


def main_kernel(
    n_chunks,
    n_lat,
    n_lon,
    tokens_hbm,
    gain_fine,
    w_qkv_fine_hbm,
    bias_fine_hbm,
    w_out_fine_hbm,
    gain_merge,
    w_merge_hbm,
    gain_coarse,
    w_qkv_coarse_hbm,
    bias_coarse_hbm,
    maps_hbm,
    coarse_maps_hbm,
    w_out_coarse_hbm,
    fine_out,
    coarse_out,
    tokens,
    w_qkv_fine,
    bias_fine,
    w_out_fine,
    w_merge,
    w_qkv_coarse,
    bias_coarse,
    w_out_coarse,
    maps,
    cmaps,
    fine_recv,
    xn,
    qkv,
    win_heads,
    heads_send,
    heads,
    merged,
    coarse_in,
    coarse_send,
    coarse_recv,
    xn_coarse,
    qkv_coarse,
    back_send,
    back_recv,
    load_sem,
    token_sem,
    own_sem,
    fine_ssem,
    fine_rsem,
    heads_ssem,
    heads_rsem,
    coarse_ssem,
    coarse_rsem,
    back_ssem,
    back_rsem,
):
    lat = lax.axis_index("lat")
    lon = lax.axis_index("lon")
    member = (lat % 2) * 2 + lon % 2

    def at(dlat, dlon):
        return (lax.rem(lat + dlat + n_lat, n_lat), lax.rem(lon + dlon + n_lon, n_lon))

    def partner(k):
        return (
            lat + (k // 2) * (1 - 2 * (lat % 2)),
            lon + (k % 2) * (1 - 2 * (lon % 2)),
        )

    def way(c):
        return 2 * (c % 2) - 1

    def quarter(c, k):
        return 3 - k + (c % 2) * (2 * k - 3)

    def tile_part(ref, c, q):
        return ref.at[
            pl.ds(2 * c, 2), pl.ds(q // 2 * HALF_R, HALF_R), pl.ds(q % 2 * HALF_C, HALF_C)
        ]

    def fine_copy(c, k):
        q = quarter(c, k)
        return pltpu.make_async_remote_copy(
            tile_part(tokens_hbm, c, q),
            fine_recv.at[c, q],
            fine_ssem.at[c, k],
            fine_rsem.at[c, k],
            device_id=at(k // 2 * way(c), k % 2 * way(c)),
            device_id_type=MESH,
        )

    def own_copy(c):
        q = quarter(c, 0)
        return pltpu.make_async_copy(
            tile_part(tokens_hbm, c, q), fine_recv.at[c, q], own_sem.at[c]
        )

    def heads_copy(c, k):
        q = quarter(c, k)
        return pltpu.make_async_remote_copy(
            heads_send.at[c, q],
            tile_part(heads, c, q),
            heads_ssem.at[c, k],
            heads_rsem.at[c, k],
            device_id=at(-(k // 2) * way(c), -(k % 2) * way(c)),
            device_id_type=MESH,
        )

    def other(k):
        mine_lat, mine_lon = lat % 2, lon % 2
        to_lat = mine_lat + (k // 2) * (1 - 2 * mine_lat)
        to_lon = mine_lon + (k % 2) * (1 - 2 * mine_lon)
        return to_lat * 2 + to_lon

    def group_copy(c, k, send, recv, ssem, rsem):
        return pltpu.make_async_remote_copy(
            send.at[c, other(k)],
            recv.at[c, member],
            ssem.at[c, k],
            rsem.at[c, k],
            device_id=partner(k),
            device_id_type=MESH,
        )

    def coarse_copy(c, k):
        return group_copy(c, k, coarse_send, coarse_recv, coarse_ssem, coarse_rsem)

    def back_copy(c, k):
        return group_copy(c, k, back_send, back_recv, back_ssem, back_rsem)

    def token_copy(c):
        part = pl.ds(2 * c, 2)
        return pltpu.make_async_copy(tokens_hbm.at[part], tokens.at[part], token_sem.at[c])

    def load(n, src, dst):
        return pltpu.make_async_copy(src, dst, load_sem.at[n])

    loads = [
        load(0, maps_hbm, maps),
        load(1, w_qkv_fine_hbm, w_qkv_fine),
        load(2, bias_fine_hbm, bias_fine.at[0]),
        load(3, w_out_fine_hbm, w_out_fine),
        load(4, w_merge_hbm, w_merge),
        load(5, coarse_maps_hbm, cmaps),
        load(6, w_qkv_coarse_hbm, w_qkv_coarse),
        load(7, bias_coarse_hbm, bias_coarse),
        load(8, w_out_coarse_hbm, w_out_coarse),
    ]

    barrier = pltpu.get_barrier_semaphore()
    for near in (at(0, -1), at(0, 1), at(-1, 0), at(1, 0), at(-1, -1), at(1, 1), partner(3)):
        pl.semaphore_signal(barrier, inc=1, device_id=near, device_id_type=MESH)
    pl.semaphore_wait(barrier, 7)

    def send_tokens(c, _):
        for k in (3, 2, 1):
            fine_copy(c, k).start()
        own_copy(c).start()
        return 0

    lax.fori_loop(0, AHEAD, send_tokens, 0)
    for copy in loads[:3]:
        copy.start()
    for c in range(n_chunks):
        token_copy(c).start()
    for copy in loads[3:]:
        copy.start()

    loads[2].wait()
    token_q = lax.broadcasted_iota(jnp.int32, (WIN, WIN), 0)
    token_k = lax.broadcasted_iota(jnp.int32, (WIN, WIN), 1)
    late_q = (token_q % (ROWS * COLS)) >= HALF_R * COLS
    late_k = (token_k % (ROWS * COLS)) >= HALF_R * COLS
    mask = jnp.where(late_q == late_k, 0.0, NEG)
    for h in range(D1 // HS):
        bias_fine[1, h] = bias_fine[0, h] + mask
    loads[0].wait()
    loads[1].wait()

    def fine_attention(c):
        own_copy(c).wait()
        for k in (1, 2, 3):
            fine_copy(c, k).wait_recv()

        @pl.when(c + AHEAD < n_chunks)
        def _():
            send_tokens(c + AHEAD, 0)

        for b in range(2):
            rows = fine_recv[c, :, b].reshape(PAIR, D1)
            xn[pl.ds(b * PAIR, PAIR)] = normed(dot(maps[0], rows), gain_fine[...])
        for n in range(3):
            part = dot(xn[...], w_qkv_fine[:, n * D1 : (n + 1) * D1]).astype(jnp.bfloat16)
            if n == 0:
                part = part * jnp.bfloat16(HS**-0.5)
            qkv[:, n * D1 : (n + 1) * D1] = part
        at_edge = lat == (1 - c % 2) * (n_lat - 1)
        which = jnp.where(at_edge, 1, 0)

        def window(w, _):
            rows = pl.ds(pl.multiple_of(w * WIN, 16), WIN)
            for pair in range(D1 // 128):
                lanes = [pl.ds(n * D1 + pair * 128, 128) for n in range(3)]
                win_heads[rows, lanes[0]] = attend_pair(
                    qkv[rows, lanes[0]],
                    qkv[rows, lanes[1]],
                    qkv[rows, lanes[2]],
                    bias_fine[which, 2 * pair],
                    bias_fine[which, 2 * pair + 1],
                )
            return 0

        lax.fori_loop(0, NW, window, 0)
        for b in range(2):
            rows = dot(maps[1], win_heads[pl.ds(b * PAIR, PAIR)]).astype(jnp.bfloat16)
            heads_send[c, :, b] = rows.reshape(4, HALF_R, HALF_C, LEVELS, D1)
        for k in (3, 2, 1):
            heads_copy(c, k).start()
        own = quarter(c, 0)
        tile_part(heads, c, own)[...] = heads_send[c, own]

    def merge(c):
        @pl.when(c == 0)
        def _():
            loads[3].wait()
            loads[4].wait()
            loads[5].wait()

        token_copy(c).wait()
        for k in (1, 2, 3):
            heads_copy(c, k).wait_recv()
        part = pl.ds(2 * c, 2)
        rows = dot(heads[part].reshape(4 * CROWS, D1), w_out_fine[...])
        rows = rows + tokens[part].reshape(4 * CROWS, D1).astype(jnp.float32)
        fine_out[part] = rows.reshape(2, HALF_R, 2, HALF_C, 2, LEVELS, D1)
        total = jnp.zeros((CROWS, 1), jnp.float32)
        for g in range(4):
            values = fine_out[part, :, g % 2, :, g // 2].reshape(CROWS, D1)
            total = total + jnp.sum(values, axis=-1, keepdims=True)
        average = total / (4 * D1)
        total = jnp.zeros((CROWS, 1), jnp.float32)
        for g in range(4):
            centred = fine_out[part, :, g % 2, :, g // 2].reshape(CROWS, D1) - average
            total = total + jnp.sum(centred * centred, axis=-1, keepdims=True)
        inverse = lax.rsqrt(total / (4 * D1) + EPS)
        for g in range(4):
            lanes = pl.ds(g * D1, D1)
            centred = fine_out[part, :, g % 2, :, g // 2].reshape(CROWS, D1) - average
            merged[:, lanes] = (centred * inverse * gain_merge[:, lanes]).astype(jnp.bfloat16)
        coarse = dot(merged[...], w_merge[...]).astype(jnp.bfloat16)
        coarse_in[c] = coarse
        rows = dot(cmaps[TO_SEND], coarse).astype(jnp.bfloat16)
        coarse_send[c] = rows.reshape(coarse_send.shape[1:])
        for k in (3, 2, 1):
            coarse_copy(c, k).start()
        coarse_recv[c, member] = coarse_send[c, member]

    def coarse_attention(c):
        @pl.when(c == 0)
        def _():
            loads[6].wait()
            loads[7].wait()

        for k in (1, 2, 3):
            coarse_copy(c, k).wait_recv()
        values = dot(cmaps[TO_WIN], coarse_recv[c].reshape(WIN, D2))
        xn_coarse[...] = normed(values, gain_coarse[...])
        for n in range(3):
            lanes = pl.ds(n * D2, D2)
            part = dot(xn_coarse[...], w_qkv_coarse[:, lanes]).astype(jnp.bfloat16)
            if n == 0:
                part = part * jnp.bfloat16(HS**-0.5)
            qkv_coarse[:, lanes] = part
        results = []
        for pair in range(D2 // 128):
            lanes = [pl.ds(n * D2 + pair * 128, 128) for n in range(3)]
            results.append(
                attend_pair(
                    qkv_coarse[:, lanes[0]],
                    qkv_coarse[:, lanes[1]],
                    qkv_coarse[:, lanes[2]],
                    bias_coarse[2 * pair],
                    bias_coarse[2 * pair + 1],
                )
            )
        rows = dot(cmaps[FROM_WIN], jnp.concatenate(results, axis=1)).astype(jnp.bfloat16)
        back_send[c] = rows.reshape(back_send.shape[1:])
        for k in (3, 2, 1):
            back_copy(c, k).start()
        back_recv[c, member] = back_send[c, member]

    def finish(c):
        @pl.when(c == 0)
        def _():
            loads[8].wait()

        for k in (1, 2, 3):
            back_copy(c, k).wait_recv()
        rows = dot(cmaps[FROM_SEND], back_recv[c].reshape(CROWS, D2)).astype(jnp.bfloat16)
        rows = dot(rows, w_out_coarse[...]) + coarse_in[c].astype(jnp.float32)
        coarse_out[pl.ds(2 * c, 2)] = rows.reshape(2, HALF_R, HALF_C, LEVELS, D2)

    def step(s, _):
        for depth, stage in zip(BEHIND, (fine_attention, merge, coarse_attention, finish)):

            @pl.when((s >= depth) & (s < n_chunks + depth))
            def _():
                stage(s - depth)

        return 0

    lax.fori_loop(0, n_chunks + BEHIND[-1], step, 0)

    def drain(c, _):
        for k in (1, 2, 3):
            fine_copy(c, k).wait_send()
            heads_copy(c, k).wait_send()
            coarse_copy(c, k).wait_send()
            back_copy(c, k).wait_send()
        return 0

    lax.fori_loop(0, n_chunks, drain, 0)


def body(
    fine_tokens,
    gain_fine,
    w_qkv_fine,
    bias_fine,
    w_out_fine,
    gain_merge,
    w_merge,
    gain_coarse,
    w_qkv_coarse,
    bias_coarse,
    w_out_coarse,
):
    tokens = fine_tokens.transpose(0, 2, 3, 1, 4)
    batch = tokens.shape[0]
    chunks = batch // 2
    bf16, f32 = jnp.bfloat16, jnp.float32
    maps = jnp.asarray(pair_maps(), bf16)
    cmaps = jnp.asarray(coarse_maps(), bf16)
    hbm = pl.BlockSpec(memory_space=pl.ANY)
    vmem = pl.BlockSpec(memory_space=pltpu.VMEM)
    dma = pltpu.SemaphoreType.DMA
    slots = (chunks, NW, CROWS // NW // 4, 4, D2)
    fine_out, coarse_out = pl.pallas_call(
        functools.partial(main_kernel, chunks, lax.axis_size("lat"), lax.axis_size("lon")),
        out_shape=(
            pltpu.VMEM((batch, HALF_R, 2, HALF_C, 2, LEVELS, D1), f32),
            pltpu.VMEM((batch, HALF_R, HALF_C, LEVELS, D2), f32),
        ),
        in_specs=[hbm, vmem, hbm, hbm, hbm, vmem, hbm, vmem, hbm, hbm, hbm, hbm, hbm],
        out_specs=(vmem, vmem),
        scratch_shapes=[
            pltpu.VMEM(tokens.shape, bf16),
            pltpu.VMEM(w_qkv_fine.shape, bf16),
            pltpu.VMEM((2,) + bias_fine.shape, f32),
            pltpu.VMEM(w_out_fine.shape, bf16),
            pltpu.VMEM(w_merge.shape, bf16),
            pltpu.VMEM(w_qkv_coarse.shape, bf16),
            pltpu.VMEM(bias_coarse.shape, f32),
            pltpu.VMEM(w_out_coarse.shape, bf16),
            pltpu.VMEM(maps.shape, bf16),
            pltpu.VMEM(cmaps.shape, bf16),
            pltpu.VMEM((chunks, 4, 2, HALF_R, HALF_C, LEVELS, D1), bf16),
            pltpu.VMEM((NW * WIN, D1), bf16),
            pltpu.VMEM((NW * WIN, 3 * D1), bf16),
            pltpu.VMEM((NW * WIN, D1), bf16),
            pltpu.VMEM((chunks, 4, 2, HALF_R, HALF_C, LEVELS, D1), bf16),
            pltpu.VMEM(tokens.shape, bf16),
            pltpu.VMEM((CROWS, 4 * D1), bf16),
            pltpu.VMEM((chunks, CROWS, D2), bf16),
            pltpu.VMEM(slots, bf16),
            pltpu.VMEM(slots, bf16),
            pltpu.VMEM((WIN, D2), bf16),
            pltpu.VMEM((WIN, 3 * D2), bf16),
            pltpu.VMEM(slots, bf16),
            pltpu.VMEM(slots, bf16),
            dma((9,)),
            dma((chunks,)),
            dma((chunks,)),
        ]
        + [dma((chunks, 4)) for _ in range(8)],
        compiler_params=pltpu.CompilerParams(
            collective_id=0, has_side_effects=True, vmem_limit_bytes=VMEM_LIMIT
        ),
        name="window_levels",
    )(
        tokens,
        gain_fine[None],
        w_qkv_fine,
        bias_fine,
        w_out_fine,
        gain_merge[None],
        w_merge,
        gain_coarse[None],
        w_qkv_coarse,
        bias_coarse,
        maps,
        cmaps,
        w_out_coarse,
    )
    fine_out = fine_out.reshape(tokens.shape)
    return fine_out.transpose(0, 3, 1, 2, 4), coarse_out.transpose(0, 3, 1, 2, 4)


def solution(mesh):
    tile = P(None, None, "lat", "lon", None)
    return jax.shard_map(
        body,
        mesh=mesh,
        in_specs=(tile,) + (P(),) * 10,
        out_specs=(tile, tile),
        check_vma=False,
    )
```

```python
import functools

import jax
import jax.numpy as jnp
import numpy as np
from jax import lax
from jax.experimental import pallas as pl
from jax.experimental.pallas import tpu as pltpu
from jax.sharding import PartitionSpec as P

EPS = 1e-05
NEG = -1e30
ROWS, COLS, LEVELS, WLEV, HS = 6, 12, 4, 2, 64
HALF_R, HALF_C = ROWS // 2, COLS // 2
WIN = WLEV * ROWS * COLS
PAIR = 2 * WIN
NW = 4
BEHIND = (0, 2, 4, 5)
AHEAD = 2
CROWS = 2 * HALF_R * HALF_C * LEVELS
D1, D2 = 512, 1024
TO_SEND, TO_WIN, FROM_WIN, FROM_SEND = range(4)
MESH = pl.DeviceIdType.MESH
VMEM_LIMIT = 52 * 1024 * 1024


def pair_maps():
    to_win = np.zeros((PAIR, PAIR), np.float32)
    for lev in range(LEVELS):
        for r in range(ROWS):
            for c in range(COLS):
                q = (1 - r // HALF_R) * 2 + 1 - c // HALF_C
                src = ((q * HALF_R + r % HALF_R) * HALF_C + c % HALF_C) * LEVELS + lev
                win = lev // WLEV * WIN + (lev % WLEV * ROWS + r) * COLS + c
                to_win[win, src] = 1
    return np.stack([to_win, to_win.T])


def coarse_maps():
    to_send = np.zeros((CROWS, CROWS), np.float32)
    to_win = np.zeros((CROWS, CROWS), np.float32)
    part = CROWS // NW
    for b in range(2):
        for r in range(HALF_R):
            for c in range(HALF_C):
                for lev in range(LEVELS):
                    nat = ((b * HALF_R + r) * HALF_C + c) * LEVELS + lev
                    t = (lev % WLEV * HALF_R + r) * HALF_C + c
                    to_send[(b * 2 + lev // WLEV) * part + t, nat] = 1
    for lev in range(WLEV):
        for r in range(ROWS):
            for c in range(COLS):
                m = r // HALF_R * 2 + c // HALF_C
                t = (lev * HALF_R + r % HALF_R) * HALF_C + c % HALF_C
                to_win[(lev * ROWS + r) * COLS + c, m * part + t] = 1
    return np.stack([to_send, to_win, to_win.T, to_send.T])


def dot(a, b):
    return jnp.dot(a, b, preferred_element_type=jnp.float32)


def dot_t(a, b):
    return lax.dot_general(a, b, (((1,), (1,)), ((), ())), preferred_element_type=jnp.float32)


def normed(values, gain):
    average = jnp.mean(values, axis=-1, keepdims=True)
    centred = values - average
    variance = jnp.mean(centred * centred, axis=-1, keepdims=True)
    return (centred * lax.rsqrt(variance + EPS) * gain).astype(jnp.bfloat16)


def attend_all(queries, keys, values, biases):
    low = lax.broadcasted_iota(jnp.int32, (WIN, 128), 1) < HS
    zero = jnp.zeros((), jnp.bfloat16)
    ones = jnp.ones((WIN, 128), jnp.bfloat16)
    scores = [
        dot_t(jnp.concatenate([jnp.where(low, q, zero), jnp.where(low, zero, q)], axis=0), k)
        for q, k in zip(queries, keys)
    ]
    scores = [s + b for s, b in zip(scores, biases)]
    probs = [jnp.exp(s - jnp.max(s, axis=-1, keepdims=True)).astype(jnp.bfloat16) for s in scores]
    sums = [dot(p, jnp.concatenate([v, ones], axis=1)) for p, v in zip(probs, values)]
    both = jnp.concatenate([low, low], axis=1)
    picked = [jnp.where(both, s[:WIN], s[WIN:]) for s in sums]
    return [(p[:, :128] / p[:, 128:]).astype(jnp.bfloat16) for p in picked]


def main_kernel(
    n_chunks,
    n_lat,
    n_lon,
    tokens_hbm,
    gain_fine,
    w_qkv_fine_hbm,
    bias_fine_hbm,
    w_out_fine_hbm,
    gain_merge,
    w_merge_hbm,
    gain_coarse,
    w_qkv_coarse_hbm,
    bias_coarse_hbm,
    maps_hbm,
    coarse_maps_hbm,
    w_out_coarse_hbm,
    fine_out,
    coarse_out,
    tokens,
    w_qkv_fine,
    bias_fine,
    w_out_fine,
    w_merge,
    w_qkv_coarse,
    bias_coarse,
    w_out_coarse,
    maps,
    cmaps,
    fine_recv,
    xn,
    qkv,
    win_heads,
    heads_send,
    heads,
    merged,
    coarse_in,
    coarse_send,
    coarse_recv,
    xn_coarse,
    qkv_coarse,
    back_send,
    back_recv,
    load_sem,
    token_sem,
    own_sem,
    fine_ssem,
    fine_rsem,
    heads_ssem,
    heads_rsem,
    coarse_ssem,
    coarse_rsem,
    back_ssem,
    back_rsem,
):
    lat = lax.axis_index("lat")
    lon = lax.axis_index("lon")
    member = (lat % 2) * 2 + lon % 2

    def at(dlat, dlon):
        return (lax.rem(lat + dlat + n_lat, n_lat), lax.rem(lon + dlon + n_lon, n_lon))

    def partner(k):
        return (
            lat + (k // 2) * (1 - 2 * (lat % 2)),
            lon + (k % 2) * (1 - 2 * (lon % 2)),
        )

    def way(c):
        return 2 * (c % 2) - 1

    def quarter(c, k):
        return 3 - k + (c % 2) * (2 * k - 3)

    def tile_part(ref, c, q):
        return ref.at[
            pl.ds(2 * c, 2), pl.ds(q // 2 * HALF_R, HALF_R), pl.ds(q % 2 * HALF_C, HALF_C)
        ]

    def fine_copy(c, k):
        q = quarter(c, k)
        return pltpu.make_async_remote_copy(
            tile_part(tokens_hbm, c, q),
            fine_recv.at[c, q],
            fine_ssem.at[c, k],
            fine_rsem.at[c, k],
            device_id=at(k // 2 * way(c), k % 2 * way(c)),
            device_id_type=MESH,
        )

    def own_copy(c):
        q = quarter(c, 0)
        return pltpu.make_async_copy(
            tile_part(tokens_hbm, c, q), fine_recv.at[c, q], own_sem.at[c]
        )

    def heads_copy(c, k):
        q = quarter(c, k)
        return pltpu.make_async_remote_copy(
            heads_send.at[c, q],
            tile_part(heads, c, q),
            heads_ssem.at[c, k],
            heads_rsem.at[c, k],
            device_id=at(-(k // 2) * way(c), -(k % 2) * way(c)),
            device_id_type=MESH,
        )

    def other(k):
        mine_lat, mine_lon = lat % 2, lon % 2
        to_lat = mine_lat + (k // 2) * (1 - 2 * mine_lat)
        to_lon = mine_lon + (k % 2) * (1 - 2 * mine_lon)
        return to_lat * 2 + to_lon

    def group_copy(c, k, send, recv, ssem, rsem):
        return pltpu.make_async_remote_copy(
            send.at[c, other(k)],
            recv.at[c, member],
            ssem.at[c, k],
            rsem.at[c, k],
            device_id=partner(k),
            device_id_type=MESH,
        )

    def coarse_copy(c, k):
        return group_copy(c, k, coarse_send, coarse_recv, coarse_ssem, coarse_rsem)

    def back_copy(c, k):
        return group_copy(c, k, back_send, back_recv, back_ssem, back_rsem)

    def token_copy(c):
        part = pl.ds(2 * c, 2)
        return pltpu.make_async_copy(tokens_hbm.at[part], tokens.at[part], token_sem.at[c])

    def load(n, src, dst):
        return pltpu.make_async_copy(src, dst, load_sem.at[n])

    loads = [
        load(0, maps_hbm, maps),
        load(1, w_qkv_fine_hbm, w_qkv_fine),
        load(2, bias_fine_hbm, bias_fine.at[0]),
        load(3, w_out_fine_hbm, w_out_fine),
        load(4, w_merge_hbm, w_merge),
        load(5, coarse_maps_hbm, cmaps),
        load(6, w_qkv_coarse_hbm, w_qkv_coarse),
        load(7, bias_coarse_hbm, bias_coarse),
        load(8, w_out_coarse_hbm, w_out_coarse),
    ]

    barrier = pltpu.get_barrier_semaphore()
    for near in (at(0, -1), at(0, 1), at(-1, 0), at(1, 0), at(-1, -1), at(1, 1), partner(3)):
        pl.semaphore_signal(barrier, inc=1, device_id=near, device_id_type=MESH)
    pl.semaphore_wait(barrier, 7)

    def send_tokens(c, _):
        for k in (3, 2, 1):
            fine_copy(c, k).start()
        own_copy(c).start()
        return 0

    lax.fori_loop(0, AHEAD, send_tokens, 0)
    for copy in loads[:3]:
        copy.start()
    for c in range(n_chunks):
        token_copy(c).start()
    for copy in loads[3:]:
        copy.start()

    loads[2].wait()
    token_q = lax.broadcasted_iota(jnp.int32, (WIN, WIN), 0)
    token_k = lax.broadcasted_iota(jnp.int32, (WIN, WIN), 1)
    late_q = (token_q % (ROWS * COLS)) >= HALF_R * COLS
    late_k = (token_k % (ROWS * COLS)) >= HALF_R * COLS
    mask = jnp.where(late_q == late_k, 0.0, NEG)
    for h in range(D1 // HS):
        bias_fine[1, h] = bias_fine[0, h] + mask
    loads[0].wait()
    loads[1].wait()

    def fine_attention(c):
        own_copy(c).wait()
        for k in (1, 2, 3):
            fine_copy(c, k).wait_recv()

        @pl.when(c + AHEAD < n_chunks)
        def _():
            send_tokens(c + AHEAD, 0)

        for b in range(2):
            rows = fine_recv[c, :, b].reshape(PAIR, D1)
            xn[pl.ds(b * PAIR, PAIR)] = normed(dot(maps[0], rows), gain_fine[...])
        for n in range(3):
            part = dot(xn[...], w_qkv_fine[:, n * D1 : (n + 1) * D1]).astype(jnp.bfloat16)
            if n == 0:
                part = part * jnp.bfloat16(HS**-0.5)
            qkv[:, n * D1 : (n + 1) * D1] = part
        at_edge = lat == (1 - c % 2) * (n_lat - 1)
        which = jnp.where(at_edge, 1, 0)

        def window(w, _):
            rows = pl.ds(pl.multiple_of(w * WIN, 16), WIN)
            lanes = [[pl.ds(n * D1 + p * 128, 128) for p in range(D1 // 128)] for n in range(3)]
            results = attend_all(
                *([qkv[rows, lane] for lane in group] for group in lanes),
                [bias_fine[which, pl.ds(2 * p, 2)].reshape(2 * WIN, WIN) for p in range(D1 // 128)],
            )
            for lane, result in zip(lanes[0], results):
                win_heads[rows, lane] = result
            return 0

        lax.fori_loop(0, NW, window, 0, unroll=2)
        for b in range(2):
            rows = dot(maps[1], win_heads[pl.ds(b * PAIR, PAIR)]).astype(jnp.bfloat16)
            heads_send[c, :, b] = rows.reshape(4, HALF_R, HALF_C, LEVELS, D1)
        for k in (3, 2, 1):
            heads_copy(c, k).start()
        own = quarter(c, 0)
        tile_part(heads, c, own)[...] = heads_send[c, own]

    def merge(c):
        @pl.when(c == 0)
        def _():
            loads[3].wait()
            loads[4].wait()
            loads[5].wait()

        token_copy(c).wait()
        for k in (1, 2, 3):
            heads_copy(c, k).wait_recv()
        part = pl.ds(2 * c, 2)
        rows = dot(heads[part].reshape(4 * CROWS, D1), w_out_fine[...])
        rows = rows + tokens[part].reshape(4 * CROWS, D1).astype(jnp.float32)
        fine_out[part] = rows.reshape(2, HALF_R, 2, HALF_C, 2, LEVELS, D1)
        total = jnp.zeros((CROWS, 1), jnp.float32)
        for g in range(4):
            values = fine_out[part, :, g % 2, :, g // 2].reshape(CROWS, D1)
            total = total + jnp.sum(values, axis=-1, keepdims=True)
        average = total / (4 * D1)
        total = jnp.zeros((CROWS, 1), jnp.float32)
        for g in range(4):
            centred = fine_out[part, :, g % 2, :, g // 2].reshape(CROWS, D1) - average
            total = total + jnp.sum(centred * centred, axis=-1, keepdims=True)
        inverse = lax.rsqrt(total / (4 * D1) + EPS)
        for g in range(4):
            lanes = pl.ds(g * D1, D1)
            centred = fine_out[part, :, g % 2, :, g // 2].reshape(CROWS, D1) - average
            merged[:, lanes] = (centred * inverse * gain_merge[:, lanes]).astype(jnp.bfloat16)
        coarse = dot(merged[...], w_merge[...]).astype(jnp.bfloat16)
        coarse_in[c] = coarse
        rows = dot(cmaps[TO_SEND], coarse).astype(jnp.bfloat16)
        coarse_send[c] = rows.reshape(coarse_send.shape[1:])
        for k in (3, 2, 1):
            coarse_copy(c, k).start()
        coarse_recv[c, member] = coarse_send[c, member]

    def coarse_attention(c):
        @pl.when(c == 0)
        def _():
            loads[6].wait()
            loads[7].wait()

        for k in (1, 2, 3):
            coarse_copy(c, k).wait_recv()
        values = dot(cmaps[TO_WIN], coarse_recv[c].reshape(WIN, D2))
        xn_coarse[...] = normed(values, gain_coarse[...])
        for n in range(3):
            lanes = pl.ds(n * D2, D2)
            part = dot(xn_coarse[...], w_qkv_coarse[:, lanes]).astype(jnp.bfloat16)
            if n == 0:
                part = part * jnp.bfloat16(HS**-0.5)
            qkv_coarse[:, lanes] = part
        results = []
        for first in range(0, D2 // 128, 4):
            pairs = range(first, first + 4)
            lanes = [[pl.ds(n * D2 + p * 128, 128) for p in pairs] for n in range(3)]
            results += attend_all(
                *([qkv_coarse[:, lane] for lane in group] for group in lanes),
                [bias_coarse[pl.ds(2 * p, 2)].reshape(2 * WIN, WIN) for p in pairs],
            )
        rows = dot(cmaps[FROM_WIN], jnp.concatenate(results, axis=1)).astype(jnp.bfloat16)
        back_send[c] = rows.reshape(back_send.shape[1:])
        for k in (3, 2, 1):
            back_copy(c, k).start()
        back_recv[c, member] = back_send[c, member]

    def finish(c):
        @pl.when(c == 0)
        def _():
            loads[8].wait()

        for k in (1, 2, 3):
            back_copy(c, k).wait_recv()
        rows = dot(cmaps[FROM_SEND], back_recv[c].reshape(CROWS, D2)).astype(jnp.bfloat16)
        rows = dot(rows, w_out_coarse[...]) + coarse_in[c].astype(jnp.float32)
        coarse_out[pl.ds(2 * c, 2)] = rows.reshape(2, HALF_R, HALF_C, LEVELS, D2)

    def step(s, _):
        for depth, stage in zip(BEHIND, (fine_attention, merge, coarse_attention, finish)):

            @pl.when((s >= depth) & (s < n_chunks + depth))
            def _():
                stage(s - depth)

        return 0

    lax.fori_loop(0, n_chunks + BEHIND[-1], step, 0)

    def drain(c, _):
        for k in (1, 2, 3):
            fine_copy(c, k).wait_send()
            heads_copy(c, k).wait_send()
            coarse_copy(c, k).wait_send()
            back_copy(c, k).wait_send()
        return 0

    lax.fori_loop(0, n_chunks, drain, 0)


def body(
    fine_tokens,
    gain_fine,
    w_qkv_fine,
    bias_fine,
    w_out_fine,
    gain_merge,
    w_merge,
    gain_coarse,
    w_qkv_coarse,
    bias_coarse,
    w_out_coarse,
):
    tokens = fine_tokens.transpose(0, 2, 3, 1, 4)
    batch = tokens.shape[0]
    chunks = batch // 2
    bf16, f32 = jnp.bfloat16, jnp.float32
    maps = jnp.asarray(pair_maps(), bf16)
    cmaps = jnp.asarray(coarse_maps(), bf16)
    hbm = pl.BlockSpec(memory_space=pl.ANY)
    vmem = pl.BlockSpec(memory_space=pltpu.VMEM)
    dma = pltpu.SemaphoreType.DMA
    slots = (chunks, NW, CROWS // NW // 4, 4, D2)
    fine_out, coarse_out = pl.pallas_call(
        functools.partial(main_kernel, chunks, lax.axis_size("lat"), lax.axis_size("lon")),
        out_shape=(
            pltpu.VMEM((batch, HALF_R, 2, HALF_C, 2, LEVELS, D1), f32),
            pltpu.VMEM((batch, HALF_R, HALF_C, LEVELS, D2), f32),
        ),
        in_specs=[hbm, vmem, hbm, hbm, hbm, vmem, hbm, vmem, hbm, hbm, hbm, hbm, hbm],
        out_specs=(vmem, vmem),
        scratch_shapes=[
            pltpu.VMEM(tokens.shape, bf16),
            pltpu.VMEM(w_qkv_fine.shape, bf16),
            pltpu.VMEM((2,) + bias_fine.shape, f32),
            pltpu.VMEM(w_out_fine.shape, bf16),
            pltpu.VMEM(w_merge.shape, bf16),
            pltpu.VMEM(w_qkv_coarse.shape, bf16),
            pltpu.VMEM(bias_coarse.shape, f32),
            pltpu.VMEM(w_out_coarse.shape, bf16),
            pltpu.VMEM(maps.shape, bf16),
            pltpu.VMEM(cmaps.shape, bf16),
            pltpu.VMEM((chunks, 4, 2, HALF_R, HALF_C, LEVELS, D1), bf16),
            pltpu.VMEM((NW * WIN, D1), bf16),
            pltpu.VMEM((NW * WIN, 3 * D1), bf16),
            pltpu.VMEM((NW * WIN, D1), bf16),
            pltpu.VMEM((chunks, 4, 2, HALF_R, HALF_C, LEVELS, D1), bf16),
            pltpu.VMEM(tokens.shape, bf16),
            pltpu.VMEM((CROWS, 4 * D1), bf16),
            pltpu.VMEM((chunks, CROWS, D2), bf16),
            pltpu.VMEM(slots, bf16),
            pltpu.VMEM(slots, bf16),
            pltpu.VMEM((WIN, D2), bf16),
            pltpu.VMEM((WIN, 3 * D2), bf16),
            pltpu.VMEM(slots, bf16),
            pltpu.VMEM(slots, bf16),
            dma((9,)),
            dma((chunks,)),
            dma((chunks,)),
        ]
        + [dma((chunks, 4)) for _ in range(8)],
        compiler_params=pltpu.CompilerParams(
            collective_id=0, has_side_effects=True, vmem_limit_bytes=VMEM_LIMIT
        ),
        name="window_levels",
    )(
        tokens,
        gain_fine[None],
        w_qkv_fine,
        bias_fine,
        w_out_fine,
        gain_merge[None],
        w_merge,
        gain_coarse[None],
        w_qkv_coarse,
        bias_coarse,
        maps,
        cmaps,
        w_out_coarse,
    )
    fine_out = fine_out.reshape(tokens.shape)
    return fine_out.transpose(0, 3, 1, 2, 4), coarse_out.transpose(0, 3, 1, 2, 4)


def solution(mesh):
    tile = P(None, None, "lat", "lon", None)
    return jax.shard_map(
        body,
        mesh=mesh,
        in_specs=(tile,) + (P(),) * 10,
        out_specs=(tile, tile),
        check_vma=False,
    )
```

```python
import functools

import jax
import jax.numpy as jnp
import numpy as np
from jax import lax
from jax.experimental import pallas as pl
from jax.experimental.pallas import tpu as pltpu
from jax.sharding import PartitionSpec as P

EPS = 1e-05
NEG = -1e30
ROWS, COLS, LEVELS, WLEV, HS = 6, 12, 4, 2, 64
HALF_R, HALF_C = ROWS // 2, COLS // 2
WIN = WLEV * ROWS * COLS
PAIR = 2 * WIN
NW = 4
BEHIND = (0, 1, 3, 5)
AHEAD = 2
CROWS = 2 * HALF_R * HALF_C * LEVELS
D1, D2 = 512, 1024
TO_SEND, TO_WIN, FROM_WIN, FROM_SEND = range(4)
MESH = pl.DeviceIdType.MESH
VMEM_LIMIT = 52 * 1024 * 1024


def pair_maps():
    to_win = np.zeros((PAIR, PAIR), np.float32)
    for lev in range(LEVELS):
        for r in range(ROWS):
            for c in range(COLS):
                q = (1 - r // HALF_R) * 2 + 1 - c // HALF_C
                src = ((q * HALF_R + r % HALF_R) * HALF_C + c % HALF_C) * LEVELS + lev
                win = lev // WLEV * WIN + (lev % WLEV * ROWS + r) * COLS + c
                to_win[win, src] = 1
    return np.stack([to_win, to_win.T])


def coarse_maps():
    to_send = np.zeros((CROWS, CROWS), np.float32)
    to_win = np.zeros((CROWS, CROWS), np.float32)
    part = CROWS // NW
    for b in range(2):
        for r in range(HALF_R):
            for c in range(HALF_C):
                for lev in range(LEVELS):
                    nat = ((b * HALF_R + r) * HALF_C + c) * LEVELS + lev
                    t = (lev % WLEV * HALF_R + r) * HALF_C + c
                    to_send[(b * 2 + lev // WLEV) * part + t, nat] = 1
    for lev in range(WLEV):
        for r in range(ROWS):
            for c in range(COLS):
                m = r // HALF_R * 2 + c // HALF_C
                t = (lev * HALF_R + r % HALF_R) * HALF_C + c % HALF_C
                to_win[(lev * ROWS + r) * COLS + c, m * part + t] = 1
    return np.stack([to_send, to_win, to_win.T, to_send.T])


def dot(a, b):
    return jnp.dot(a, b, preferred_element_type=jnp.float32)


def dot_t(a, b):
    return lax.dot_general(a, b, (((1,), (1,)), ((), ())), preferred_element_type=jnp.float32)


def normed(values, gain):
    average = jnp.mean(values, axis=-1, keepdims=True)
    centred = values - average
    variance = jnp.mean(centred * centred, axis=-1, keepdims=True)
    return (centred * lax.rsqrt(variance + EPS) * gain).astype(jnp.bfloat16)


def attend_all(queries, keys, values, biases):
    low = lax.broadcasted_iota(jnp.int32, (WIN, 128), 1) < HS
    zero = jnp.zeros((), jnp.bfloat16)
    ones = jnp.ones((WIN, 128), jnp.bfloat16)
    scores = [
        dot_t(jnp.concatenate([jnp.where(low, q, zero), jnp.where(low, zero, q)], axis=0), k)
        for q, k in zip(queries, keys)
    ]
    scores = [s + b for s, b in zip(scores, biases)]
    probs = [jnp.exp(s - jnp.max(s, axis=-1, keepdims=True)).astype(jnp.bfloat16) for s in scores]
    sums = [dot(p, jnp.concatenate([v, ones], axis=1)) for p, v in zip(probs, values)]
    both = jnp.concatenate([low, low], axis=1)
    picked = [jnp.where(both, s[:WIN], s[WIN:]) for s in sums]
    return [(p[:, :128] / p[:, 128:]).astype(jnp.bfloat16) for p in picked]


def main_kernel(
    n_chunks,
    n_lat,
    n_lon,
    tokens_hbm,
    gain_fine,
    w_qkv_fine_hbm,
    bias_fine_hbm,
    w_out_fine_hbm,
    gain_merge,
    w_merge_hbm,
    gain_coarse,
    w_qkv_coarse_hbm,
    bias_coarse_hbm,
    maps_hbm,
    coarse_maps_hbm,
    w_out_coarse_hbm,
    fine_out,
    coarse_out,
    tokens,
    w_qkv_fine,
    bias_fine,
    w_out_fine,
    w_merge,
    w_qkv_coarse,
    bias_coarse,
    w_out_coarse,
    maps,
    cmaps,
    fine_recv,
    xn,
    qkv,
    win_heads,
    heads_send,
    heads,
    merged,
    coarse_in,
    coarse_send,
    coarse_recv,
    xn_coarse,
    qkv_coarse,
    back_send,
    back_recv,
    load_sem,
    token_sem,
    own_sem,
    fine_ssem,
    fine_rsem,
    heads_ssem,
    heads_rsem,
    coarse_ssem,
    coarse_rsem,
    back_ssem,
    back_rsem,
):
    lat = lax.axis_index("lat")
    lon = lax.axis_index("lon")
    member = (lat % 2) * 2 + lon % 2

    def at(dlat, dlon):
        return (lax.rem(lat + dlat + n_lat, n_lat), lax.rem(lon + dlon + n_lon, n_lon))

    def partner(k):
        return (
            lat + (k // 2) * (1 - 2 * (lat % 2)),
            lon + (k % 2) * (1 - 2 * (lon % 2)),
        )

    def way(c):
        return 2 * (c % 2) - 1

    def quarter(c, k):
        return 3 - k + (c % 2) * (2 * k - 3)

    def tile_part(ref, c, q):
        return ref.at[
            pl.ds(2 * c, 2), pl.ds(q // 2 * HALF_R, HALF_R), pl.ds(q % 2 * HALF_C, HALF_C)
        ]

    def fine_copy(c, k):
        q = quarter(c, k)
        return pltpu.make_async_remote_copy(
            tile_part(tokens_hbm, c, q),
            fine_recv.at[c, q],
            fine_ssem.at[c, k],
            fine_rsem.at[c, k],
            device_id=at(k // 2 * way(c), k % 2 * way(c)),
            device_id_type=MESH,
        )

    def own_copy(c):
        q = quarter(c, 0)
        return pltpu.make_async_copy(
            tile_part(tokens_hbm, c, q), fine_recv.at[c, q], own_sem.at[c]
        )

    def heads_copy(c, k):
        q = quarter(c, k)
        return pltpu.make_async_remote_copy(
            heads_send.at[c, q],
            tile_part(heads, c, q),
            heads_ssem.at[c, k],
            heads_rsem.at[c, k],
            device_id=at(-(k // 2) * way(c), -(k % 2) * way(c)),
            device_id_type=MESH,
        )

    def other(k):
        mine_lat, mine_lon = lat % 2, lon % 2
        to_lat = mine_lat + (k // 2) * (1 - 2 * mine_lat)
        to_lon = mine_lon + (k % 2) * (1 - 2 * mine_lon)
        return to_lat * 2 + to_lon

    def group_copy(c, k, send, recv, ssem, rsem):
        return pltpu.make_async_remote_copy(
            send.at[c, other(k)],
            recv.at[c, member],
            ssem.at[c, k],
            rsem.at[c, k],
            device_id=partner(k),
            device_id_type=MESH,
        )

    def coarse_copy(c, k):
        return group_copy(c, k, coarse_send, coarse_recv, coarse_ssem, coarse_rsem)

    def back_copy(c, k):
        return group_copy(c, k, back_send, back_recv, back_ssem, back_rsem)

    def token_copy(c):
        part = pl.ds(2 * c, 2)
        return pltpu.make_async_copy(tokens_hbm.at[part], tokens.at[part], token_sem.at[c])

    def load(n, src, dst):
        return pltpu.make_async_copy(src, dst, load_sem.at[n])

    loads = [
        load(0, maps_hbm, maps),
        load(1, w_qkv_fine_hbm, w_qkv_fine),
        load(2, bias_fine_hbm, bias_fine.at[0]),
        load(3, w_out_fine_hbm, w_out_fine),
        load(4, w_merge_hbm, w_merge),
        load(5, coarse_maps_hbm, cmaps),
        load(6, w_qkv_coarse_hbm, w_qkv_coarse),
        load(7, bias_coarse_hbm, bias_coarse),
        load(8, w_out_coarse_hbm, w_out_coarse),
    ]

    barrier = pltpu.get_barrier_semaphore()
    for near in (at(0, -1), at(0, 1), at(-1, 0), at(1, 0), at(-1, -1), at(1, 1), partner(3)):
        pl.semaphore_signal(barrier, inc=1, device_id=near, device_id_type=MESH)
    pl.semaphore_wait(barrier, 7)

    def send_tokens(c, _):
        for k in (3, 2, 1):
            fine_copy(c, k).start()
        own_copy(c).start()
        return 0

    lax.fori_loop(0, AHEAD, send_tokens, 0)
    for copy in loads[:3]:
        copy.start()
    for c in range(n_chunks):
        token_copy(c).start()
    for copy in loads[3:]:
        copy.start()

    loads[2].wait()
    token_q = lax.broadcasted_iota(jnp.int32, (WIN, WIN), 0)
    token_k = lax.broadcasted_iota(jnp.int32, (WIN, WIN), 1)
    late_q = (token_q % (ROWS * COLS)) >= HALF_R * COLS
    late_k = (token_k % (ROWS * COLS)) >= HALF_R * COLS
    mask = jnp.where(late_q == late_k, 0.0, NEG)
    for h in range(D1 // HS):
        bias_fine[1, h] = bias_fine[0, h] + mask
    loads[0].wait()
    loads[1].wait()

    def fine_attention(c):
        own_copy(c).wait()
        for k in (1, 2, 3):
            fine_copy(c, k).wait_recv()

        @pl.when(c + AHEAD < n_chunks)
        def _():
            send_tokens(c + AHEAD, 0)

        for b in range(2):
            rows = fine_recv[c, :, b].reshape(PAIR, D1)
            xn[pl.ds(b * PAIR, PAIR)] = normed(dot(maps[0], rows), gain_fine[...])
        for n in range(3):
            part = dot(xn[...], w_qkv_fine[:, n * D1 : (n + 1) * D1]).astype(jnp.bfloat16)
            if n == 0:
                part = part * jnp.bfloat16(HS**-0.5)
            qkv[:, n * D1 : (n + 1) * D1] = part
        at_edge = lat == (1 - c % 2) * (n_lat - 1)
        which = jnp.where(at_edge, 1, 0)

        def window(w, _):
            rows = pl.ds(pl.multiple_of(w * WIN, 16), WIN)
            lanes = [[pl.ds(n * D1 + p * 128, 128) for p in range(D1 // 128)] for n in range(3)]
            results = attend_all(
                *([qkv[rows, lane] for lane in group] for group in lanes),
                [bias_fine[which, pl.ds(2 * p, 2)].reshape(2 * WIN, WIN) for p in range(D1 // 128)],
            )
            for lane, result in zip(lanes[0], results):
                win_heads[rows, lane] = result
            return 0

        lax.fori_loop(0, NW, window, 0, unroll=2)
        for b in range(2):
            rows = dot(maps[1], win_heads[pl.ds(b * PAIR, PAIR)]).astype(jnp.bfloat16)
            heads_send[c, :, b] = rows.reshape(4, HALF_R, HALF_C, LEVELS, D1)
        for k in (3, 2, 1):
            heads_copy(c, k).start()
        own = quarter(c, 0)
        tile_part(heads, c, own)[...] = heads_send[c, own]

    def merge(c):
        @pl.when(c == 0)
        def _():
            loads[3].wait()
            loads[4].wait()
            loads[5].wait()

        token_copy(c).wait()
        for k in (1, 2, 3):
            heads_copy(c, k).wait_recv()
        part = pl.ds(2 * c, 2)
        rows = dot(heads[part].reshape(4 * CROWS, D1), w_out_fine[...])
        rows = rows + tokens[part].reshape(4 * CROWS, D1).astype(jnp.float32)
        fine_out[part] = rows.reshape(2, HALF_R, 2, HALF_C, 2, LEVELS, D1)
        total = jnp.zeros((CROWS, 1), jnp.float32)
        for g in range(4):
            values = fine_out[part, :, g % 2, :, g // 2].reshape(CROWS, D1)
            total = total + jnp.sum(values, axis=-1, keepdims=True)
        average = total / (4 * D1)
        total = jnp.zeros((CROWS, 1), jnp.float32)
        for g in range(4):
            centred = fine_out[part, :, g % 2, :, g // 2].reshape(CROWS, D1) - average
            total = total + jnp.sum(centred * centred, axis=-1, keepdims=True)
        inverse = lax.rsqrt(total / (4 * D1) + EPS)
        for g in range(4):
            lanes = pl.ds(g * D1, D1)
            centred = fine_out[part, :, g % 2, :, g // 2].reshape(CROWS, D1) - average
            merged[:, lanes] = (centred * inverse * gain_merge[:, lanes]).astype(jnp.bfloat16)
        coarse = dot(merged[...], w_merge[...]).astype(jnp.bfloat16)
        coarse_in[c] = coarse
        rows = dot(cmaps[TO_SEND], coarse).astype(jnp.bfloat16)
        coarse_send[c] = rows.reshape(coarse_send.shape[1:])
        for k in (3, 2, 1):
            coarse_copy(c, k).start()
        coarse_recv[c, member] = coarse_send[c, member]

    def coarse_attention(c):
        @pl.when(c == 0)
        def _():
            loads[6].wait()
            loads[7].wait()

        for k in (1, 2, 3):
            coarse_copy(c, k).wait_recv()
        values = dot(cmaps[TO_WIN], coarse_recv[c].reshape(WIN, D2))
        xn_coarse[...] = normed(values, gain_coarse[...])
        for n in range(3):
            lanes = pl.ds(n * D2, D2)
            part = dot(xn_coarse[...], w_qkv_coarse[:, lanes]).astype(jnp.bfloat16)
            if n == 0:
                part = part * jnp.bfloat16(HS**-0.5)
            qkv_coarse[:, lanes] = part
        results = []
        for first in range(0, D2 // 128, 4):
            pairs = range(first, first + 4)
            lanes = [[pl.ds(n * D2 + p * 128, 128) for p in pairs] for n in range(3)]
            results += attend_all(
                *([qkv_coarse[:, lane] for lane in group] for group in lanes),
                [bias_coarse[pl.ds(2 * p, 2)].reshape(2 * WIN, WIN) for p in pairs],
            )
        rows = dot(cmaps[FROM_WIN], jnp.concatenate(results, axis=1)).astype(jnp.bfloat16)
        back_send[c] = rows.reshape(back_send.shape[1:])
        for k in (3, 2, 1):
            back_copy(c, k).start()
        back_recv[c, member] = back_send[c, member]

    def finish(c):
        @pl.when(c == 0)
        def _():
            loads[8].wait()

        for k in (1, 2, 3):
            back_copy(c, k).wait_recv()
        rows = dot(cmaps[FROM_SEND], back_recv[c].reshape(CROWS, D2)).astype(jnp.bfloat16)
        rows = dot(rows, w_out_coarse[...]) + coarse_in[c].astype(jnp.float32)
        coarse_out[pl.ds(2 * c, 2)] = rows.reshape(2, HALF_R, HALF_C, LEVELS, D2)

    def step(s, _):
        for depth, stage in zip(BEHIND, (fine_attention, merge, coarse_attention, finish)):

            @pl.when((s >= depth) & (s < n_chunks + depth))
            def _():
                stage(s - depth)

        return 0

    lax.fori_loop(0, n_chunks + BEHIND[-1], step, 0)

    def drain(c, _):
        for k in (1, 2, 3):
            fine_copy(c, k).wait_send()
            heads_copy(c, k).wait_send()
            coarse_copy(c, k).wait_send()
            back_copy(c, k).wait_send()
        return 0

    lax.fori_loop(0, n_chunks, drain, 0)


def body(
    fine_tokens,
    gain_fine,
    w_qkv_fine,
    bias_fine,
    w_out_fine,
    gain_merge,
    w_merge,
    gain_coarse,
    w_qkv_coarse,
    bias_coarse,
    w_out_coarse,
):
    tokens = fine_tokens.transpose(0, 2, 3, 1, 4)
    batch = tokens.shape[0]
    chunks = batch // 2
    bf16, f32 = jnp.bfloat16, jnp.float32
    maps = jnp.asarray(pair_maps(), bf16)
    cmaps = jnp.asarray(coarse_maps(), bf16)
    hbm = pl.BlockSpec(memory_space=pl.ANY)
    vmem = pl.BlockSpec(memory_space=pltpu.VMEM)
    dma = pltpu.SemaphoreType.DMA
    slots = (chunks, NW, CROWS // NW // 4, 4, D2)
    fine_out, coarse_out = pl.pallas_call(
        functools.partial(main_kernel, chunks, lax.axis_size("lat"), lax.axis_size("lon")),
        out_shape=(
            pltpu.VMEM((batch, HALF_R, 2, HALF_C, 2, LEVELS, D1), f32),
            pltpu.VMEM((batch, HALF_R, HALF_C, LEVELS, D2), f32),
        ),
        in_specs=[hbm, vmem, hbm, hbm, hbm, vmem, hbm, vmem, hbm, hbm, hbm, hbm, hbm],
        out_specs=(vmem, vmem),
        scratch_shapes=[
            pltpu.VMEM(tokens.shape, bf16),
            pltpu.VMEM(w_qkv_fine.shape, bf16),
            pltpu.VMEM((2,) + bias_fine.shape, f32),
            pltpu.VMEM(w_out_fine.shape, bf16),
            pltpu.VMEM(w_merge.shape, bf16),
            pltpu.VMEM(w_qkv_coarse.shape, bf16),
            pltpu.VMEM(bias_coarse.shape, f32),
            pltpu.VMEM(w_out_coarse.shape, bf16),
            pltpu.VMEM(maps.shape, bf16),
            pltpu.VMEM(cmaps.shape, bf16),
            pltpu.VMEM((chunks, 4, 2, HALF_R, HALF_C, LEVELS, D1), bf16),
            pltpu.VMEM((NW * WIN, D1), bf16),
            pltpu.VMEM((NW * WIN, 3 * D1), bf16),
            pltpu.VMEM((NW * WIN, D1), bf16),
            pltpu.VMEM((chunks, 4, 2, HALF_R, HALF_C, LEVELS, D1), bf16),
            pltpu.VMEM(tokens.shape, bf16),
            pltpu.VMEM((CROWS, 4 * D1), bf16),
            pltpu.VMEM((chunks, CROWS, D2), bf16),
            pltpu.VMEM(slots, bf16),
            pltpu.VMEM(slots, bf16),
            pltpu.VMEM((WIN, D2), bf16),
            pltpu.VMEM((WIN, 3 * D2), bf16),
            pltpu.VMEM(slots, bf16),
            pltpu.VMEM(slots, bf16),
            dma((9,)),
            dma((chunks,)),
            dma((chunks,)),
        ]
        + [dma((chunks, 4)) for _ in range(8)],
        compiler_params=pltpu.CompilerParams(
            collective_id=0, has_side_effects=True, vmem_limit_bytes=VMEM_LIMIT
        ),
        name="window_levels",
    )(
        tokens,
        gain_fine[None],
        w_qkv_fine,
        bias_fine,
        w_out_fine,
        gain_merge[None],
        w_merge,
        gain_coarse[None],
        w_qkv_coarse,
        bias_coarse,
        maps,
        cmaps,
        w_out_coarse,
    )
    fine_out = fine_out.reshape(tokens.shape)
    return fine_out.transpose(0, 3, 1, 2, 4), coarse_out.transpose(0, 3, 1, 2, 4)


def solution(mesh):
    tile = P(None, None, "lat", "lon", None)
    return jax.shard_map(
        body,
        mesh=mesh,
        in_specs=(tile,) + (P(),) * 10,
        out_specs=(tile, tile),
        check_vma=False,
    )
```

```python
import functools

import jax
import jax.numpy as jnp
import numpy as np
from jax import lax
from jax.experimental import pallas as pl
from jax.experimental.pallas import tpu as pltpu
from jax.sharding import PartitionSpec as P

EPS = 1e-05
NEG = -1e30
ROWS, COLS, LEVELS, WLEV, HS = 6, 12, 4, 2, 64
HALF_R, HALF_C = ROWS // 2, COLS // 2
WIN = WLEV * ROWS * COLS
PAIR = 2 * WIN
NW = 4
BEHIND = (0, 1, 3, 5)
AHEAD = 2
CROWS = 2 * HALF_R * HALF_C * LEVELS
D1, D2 = 512, 1024
TO_SEND, TO_WIN, FROM_WIN, FROM_SEND = range(4)
MESH = pl.DeviceIdType.MESH
VMEM_LIMIT = 52 * 1024 * 1024


def pair_maps():
    to_win = np.zeros((PAIR, PAIR), np.float32)
    for lev in range(LEVELS):
        for r in range(ROWS):
            for c in range(COLS):
                q = (1 - r // HALF_R) * 2 + 1 - c // HALF_C
                src = ((q * HALF_R + r % HALF_R) * HALF_C + c % HALF_C) * LEVELS + lev
                win = lev // WLEV * WIN + (lev % WLEV * ROWS + r) * COLS + c
                to_win[win, src] = 1
    return np.stack([to_win, to_win.T])


def coarse_maps():
    to_send = np.zeros((CROWS, CROWS), np.float32)
    to_win = np.zeros((CROWS, CROWS), np.float32)
    part = CROWS // NW
    for b in range(2):
        for r in range(HALF_R):
            for c in range(HALF_C):
                for lev in range(LEVELS):
                    nat = ((b * HALF_R + r) * HALF_C + c) * LEVELS + lev
                    t = (lev % WLEV * HALF_R + r) * HALF_C + c
                    to_send[(b * 2 + lev // WLEV) * part + t, nat] = 1
    for lev in range(WLEV):
        for r in range(ROWS):
            for c in range(COLS):
                m = r // HALF_R * 2 + c // HALF_C
                t = (lev * HALF_R + r % HALF_R) * HALF_C + c % HALF_C
                to_win[(lev * ROWS + r) * COLS + c, m * part + t] = 1
    return np.stack([to_send, to_win, to_win.T, to_send.T])


def dot(a, b):
    return jnp.dot(a, b, preferred_element_type=jnp.float32)


def dot_t(a, b):
    return lax.dot_general(a, b, (((1,), (1,)), ((), ())), preferred_element_type=jnp.float32)


def normed(values, gain):
    average = jnp.mean(values, axis=-1, keepdims=True)
    centred = values - average
    variance = jnp.mean(centred * centred, axis=-1, keepdims=True)
    return (centred * lax.rsqrt(variance + EPS) * gain).astype(jnp.bfloat16)


def attend_all(queries, keys, values, biases):
    low = lax.broadcasted_iota(jnp.int32, (WIN, 128), 1) < HS
    zero = jnp.zeros((), jnp.bfloat16)
    ones = jnp.ones((WIN, 128), jnp.bfloat16)
    scores = [
        dot_t(jnp.concatenate([jnp.where(low, q, zero), jnp.where(low, zero, q)], axis=0), k)
        for q, k in zip(queries, keys)
    ]
    scores = [s + b for s, b in zip(scores, biases)]
    probs = [jnp.exp(s - jnp.max(s, axis=-1, keepdims=True)).astype(jnp.bfloat16) for s in scores]
    sums = [dot(p, jnp.concatenate([v, ones], axis=1)) for p, v in zip(probs, values)]
    both = jnp.concatenate([low, low], axis=1)
    picked = [jnp.where(both, s[:WIN], s[WIN:]) for s in sums]
    return [(p[:, :128] / p[:, 128:]).astype(jnp.bfloat16) for p in picked]


def main_kernel(
    n_chunks,
    n_lat,
    n_lon,
    tokens_hbm,
    gain_fine,
    w_qkv_fine_hbm,
    bias_fine_hbm,
    w_out_fine_hbm,
    gain_merge,
    w_merge_hbm,
    gain_coarse,
    w_qkv_coarse_hbm,
    bias_coarse_hbm,
    maps_hbm,
    coarse_maps_hbm,
    w_out_coarse_hbm,
    fine_out,
    coarse_out,
    tokens,
    w_qkv_fine,
    bias_fine,
    w_out_fine,
    w_merge,
    w_qkv_coarse,
    bias_coarse,
    w_out_coarse,
    maps,
    cmaps,
    fine_recv,
    xn,
    qkv,
    win_heads,
    heads_send,
    heads,
    merged,
    coarse_in,
    coarse_send,
    coarse_recv,
    xn_coarse,
    qkv_coarse,
    back_send,
    back_recv,
    load_sem,
    token_sem,
    own_sem,
    fine_ssem,
    fine_rsem,
    heads_ssem,
    heads_rsem,
    coarse_ssem,
    coarse_rsem,
    back_ssem,
    back_rsem,
):
    lat = lax.axis_index("lat")
    lon = lax.axis_index("lon")
    member = (lat % 2) * 2 + lon % 2

    def at(dlat, dlon):
        return (lax.rem(lat + dlat + n_lat, n_lat), lax.rem(lon + dlon + n_lon, n_lon))

    def partner(k):
        return (
            lat + (k // 2) * (1 - 2 * (lat % 2)),
            lon + (k % 2) * (1 - 2 * (lon % 2)),
        )

    def way(c):
        return 2 * (c % 2) - 1

    def quarter(c, k):
        return 3 - k + (c % 2) * (2 * k - 3)

    def tile_part(ref, c, q):
        return ref.at[
            pl.ds(2 * c, 2), pl.ds(q // 2 * HALF_R, HALF_R), pl.ds(q % 2 * HALF_C, HALF_C)
        ]

    def fine_copy(c, k):
        q = quarter(c, k)
        return pltpu.make_async_remote_copy(
            tile_part(tokens_hbm, c, q),
            fine_recv.at[c, q],
            fine_ssem.at[c, k],
            fine_rsem.at[c, k],
            device_id=at(k // 2 * way(c), k % 2 * way(c)),
            device_id_type=MESH,
        )

    def own_copy(c):
        q = quarter(c, 0)
        return pltpu.make_async_copy(
            tile_part(tokens_hbm, c, q), fine_recv.at[c, q], own_sem.at[c]
        )

    def heads_copy(c, k):
        q = quarter(c, k)
        return pltpu.make_async_remote_copy(
            heads_send.at[c, q],
            tile_part(heads, c, q),
            heads_ssem.at[c, k],
            heads_rsem.at[c, k],
            device_id=at(-(k // 2) * way(c), -(k % 2) * way(c)),
            device_id_type=MESH,
        )

    def other(k):
        mine_lat, mine_lon = lat % 2, lon % 2
        to_lat = mine_lat + (k // 2) * (1 - 2 * mine_lat)
        to_lon = mine_lon + (k % 2) * (1 - 2 * mine_lon)
        return to_lat * 2 + to_lon

    def group_copy(c, k, send, recv, ssem, rsem):
        return pltpu.make_async_remote_copy(
            send.at[c, other(k)],
            recv.at[c, member],
            ssem.at[c, k],
            rsem.at[c, k],
            device_id=partner(k),
            device_id_type=MESH,
        )

    def coarse_copy(c, k):
        return group_copy(c, k, coarse_send, coarse_recv, coarse_ssem, coarse_rsem)

    def back_copy(c, k):
        return group_copy(c, k, back_send, back_recv, back_ssem, back_rsem)

    def token_copy(c):
        part = pl.ds(2 * c, 2)
        return pltpu.make_async_copy(tokens_hbm.at[part], tokens.at[part], token_sem.at[c])

    def load(n, src, dst):
        return pltpu.make_async_copy(src, dst, load_sem.at[n])

    loads = [
        load(0, maps_hbm, maps),
        load(1, w_qkv_fine_hbm, w_qkv_fine),
        load(2, bias_fine_hbm, bias_fine.at[0]),
        load(3, w_out_fine_hbm, w_out_fine),
        load(4, w_merge_hbm, w_merge),
        load(5, coarse_maps_hbm, cmaps),
        load(6, w_qkv_coarse_hbm, w_qkv_coarse),
        load(7, bias_coarse_hbm, bias_coarse),
        load(8, w_out_coarse_hbm, w_out_coarse),
    ]

    barrier = pltpu.get_barrier_semaphore()
    for near in (at(0, -1), at(0, 1), at(-1, 0), at(1, 0), at(-1, -1), at(1, 1), partner(3)):
        pl.semaphore_signal(barrier, inc=1, device_id=near, device_id_type=MESH)
    pl.semaphore_wait(barrier, 7)

    def send_tokens(c, _):
        for k in (3, 2, 1):
            fine_copy(c, k).start()
        own_copy(c).start()
        return 0

    lax.fori_loop(0, AHEAD, send_tokens, 0)
    for copy in loads[:3]:
        copy.start()
    for c in range(n_chunks):
        token_copy(c).start()
    for copy in loads[3:]:
        copy.start()

    loads[2].wait()
    token_q = lax.broadcasted_iota(jnp.int32, (WIN, WIN), 0)
    token_k = lax.broadcasted_iota(jnp.int32, (WIN, WIN), 1)
    late_q = (token_q % (ROWS * COLS)) >= HALF_R * COLS
    late_k = (token_k % (ROWS * COLS)) >= HALF_R * COLS
    mask = jnp.where(late_q == late_k, 0.0, NEG)
    for h in range(D1 // HS):
        bias_fine[1, h] = bias_fine[0, h] + mask
    loads[0].wait()
    loads[1].wait()

    def fine_attention(c):
        own_copy(c).wait()
        for k in (1, 2, 3):
            fine_copy(c, k).wait_recv()

        @pl.when(c + AHEAD < n_chunks)
        def _():
            send_tokens(c + AHEAD, 0)

        for b in range(2):
            rows = fine_recv[c, :, b].reshape(PAIR, D1)
            xn[pl.ds(b * PAIR, PAIR)] = normed(dot(maps[0], rows), gain_fine[...])
        for n in range(3):
            part = dot(xn[...], w_qkv_fine[:, n * D1 : (n + 1) * D1]).astype(jnp.bfloat16)
            if n == 0:
                part = part * jnp.bfloat16(HS**-0.5)
            qkv[:, n * D1 : (n + 1) * D1] = part
        at_edge = lat == (1 - c % 2) * (n_lat - 1)
        which = jnp.where(at_edge, 1, 0)

        def window(w, _):
            rows = pl.ds(pl.multiple_of(w * WIN, 16), WIN)
            lanes = [[pl.ds(n * D1 + p * 128, 128) for p in range(D1 // 128)] for n in range(3)]
            results = attend_all(
                *([qkv[rows, lane] for lane in group] for group in lanes),
                [bias_fine[which, pl.ds(2 * p, 2)].reshape(2 * WIN, WIN) for p in range(D1 // 128)],
            )
            for lane, result in zip(lanes[0], results):
                win_heads[rows, lane] = result
            return 0

        lax.fori_loop(0, NW, window, 0, unroll=4)
        for b in range(2):
            rows = dot(maps[1], win_heads[pl.ds(b * PAIR, PAIR)]).astype(jnp.bfloat16)
            heads_send[c, :, b] = rows.reshape(4, HALF_R, HALF_C, LEVELS, D1)
        for k in (3, 2, 1):
            heads_copy(c, k).start()
        own = quarter(c, 0)
        tile_part(heads, c, own)[...] = heads_send[c, own]

    def merge(c):
        @pl.when(c == 0)
        def _():
            loads[3].wait()
            loads[4].wait()
            loads[5].wait()

        token_copy(c).wait()
        for k in (1, 2, 3):
            heads_copy(c, k).wait_recv()
        part = pl.ds(2 * c, 2)
        rows = dot(heads[part].reshape(4 * CROWS, D1), w_out_fine[...])
        rows = rows + tokens[part].reshape(4 * CROWS, D1).astype(jnp.float32)
        fine_out[part] = rows.reshape(2, HALF_R, 2, HALF_C, 2, LEVELS, D1)
        total = jnp.zeros((CROWS, 1), jnp.float32)
        for g in range(4):
            values = fine_out[part, :, g % 2, :, g // 2].reshape(CROWS, D1)
            total = total + jnp.sum(values, axis=-1, keepdims=True)
        average = total / (4 * D1)
        total = jnp.zeros((CROWS, 1), jnp.float32)
        for g in range(4):
            centred = fine_out[part, :, g % 2, :, g // 2].reshape(CROWS, D1) - average
            total = total + jnp.sum(centred * centred, axis=-1, keepdims=True)
        inverse = lax.rsqrt(total / (4 * D1) + EPS)
        for g in range(4):
            lanes = pl.ds(g * D1, D1)
            centred = fine_out[part, :, g % 2, :, g // 2].reshape(CROWS, D1) - average
            merged[:, lanes] = (centred * inverse * gain_merge[:, lanes]).astype(jnp.bfloat16)
        coarse = dot(merged[...], w_merge[...]).astype(jnp.bfloat16)
        coarse_in[c] = coarse
        rows = dot(cmaps[TO_SEND], coarse).astype(jnp.bfloat16)
        coarse_send[c] = rows.reshape(coarse_send.shape[1:])
        for k in (3, 2, 1):
            coarse_copy(c, k).start()
        coarse_recv[c, member] = coarse_send[c, member]

    def coarse_attention(c):
        @pl.when(c == 0)
        def _():
            loads[6].wait()
            loads[7].wait()

        for k in (1, 2, 3):
            coarse_copy(c, k).wait_recv()
        values = dot(cmaps[TO_WIN], coarse_recv[c].reshape(WIN, D2))
        xn_coarse[...] = normed(values, gain_coarse[...])
        for n in range(3):
            lanes = pl.ds(n * D2, D2)
            part = dot(xn_coarse[...], w_qkv_coarse[:, lanes]).astype(jnp.bfloat16)
            if n == 0:
                part = part * jnp.bfloat16(HS**-0.5)
            qkv_coarse[:, lanes] = part
        results = []
        for first in range(0, D2 // 128, 4):
            pairs = range(first, first + 4)
            lanes = [[pl.ds(n * D2 + p * 128, 128) for p in pairs] for n in range(3)]
            results += attend_all(
                *([qkv_coarse[:, lane] for lane in group] for group in lanes),
                [bias_coarse[pl.ds(2 * p, 2)].reshape(2 * WIN, WIN) for p in pairs],
            )
        rows = dot(cmaps[FROM_WIN], jnp.concatenate(results, axis=1)).astype(jnp.bfloat16)
        back_send[c] = rows.reshape(back_send.shape[1:])
        for k in (3, 2, 1):
            back_copy(c, k).start()
        back_recv[c, member] = back_send[c, member]

    def finish(c):
        @pl.when(c == 0)
        def _():
            loads[8].wait()

        for k in (1, 2, 3):
            back_copy(c, k).wait_recv()
        rows = dot(cmaps[FROM_SEND], back_recv[c].reshape(CROWS, D2)).astype(jnp.bfloat16)
        rows = dot(rows, w_out_coarse[...]) + coarse_in[c].astype(jnp.float32)
        coarse_out[pl.ds(2 * c, 2)] = rows.reshape(2, HALF_R, HALF_C, LEVELS, D2)

    def step(s, _):
        for depth, stage in zip(BEHIND, (fine_attention, merge, coarse_attention, finish)):

            @pl.when((s >= depth) & (s < n_chunks + depth))
            def _():
                stage(s - depth)

        return 0

    lax.fori_loop(0, n_chunks + BEHIND[-1], step, 0)

    def drain(c, _):
        for k in (1, 2, 3):
            fine_copy(c, k).wait_send()
            heads_copy(c, k).wait_send()
            coarse_copy(c, k).wait_send()
            back_copy(c, k).wait_send()
        return 0

    lax.fori_loop(0, n_chunks, drain, 0)


def body(
    fine_tokens,
    gain_fine,
    w_qkv_fine,
    bias_fine,
    w_out_fine,
    gain_merge,
    w_merge,
    gain_coarse,
    w_qkv_coarse,
    bias_coarse,
    w_out_coarse,
):
    tokens = fine_tokens.transpose(0, 2, 3, 1, 4)
    batch = tokens.shape[0]
    chunks = batch // 2
    bf16, f32 = jnp.bfloat16, jnp.float32
    maps = jnp.asarray(pair_maps(), bf16)
    cmaps = jnp.asarray(coarse_maps(), bf16)
    hbm = pl.BlockSpec(memory_space=pl.ANY)
    vmem = pl.BlockSpec(memory_space=pltpu.VMEM)
    dma = pltpu.SemaphoreType.DMA
    slots = (chunks, NW, CROWS // NW // 4, 4, D2)
    fine_out, coarse_out = pl.pallas_call(
        functools.partial(main_kernel, chunks, lax.axis_size("lat"), lax.axis_size("lon")),
        out_shape=(
            pltpu.VMEM((batch, HALF_R, 2, HALF_C, 2, LEVELS, D1), f32),
            pltpu.VMEM((batch, HALF_R, HALF_C, LEVELS, D2), f32),
        ),
        in_specs=[hbm, vmem, hbm, hbm, hbm, vmem, hbm, vmem, hbm, hbm, hbm, hbm, hbm],
        out_specs=(vmem, vmem),
        scratch_shapes=[
            pltpu.VMEM(tokens.shape, bf16),
            pltpu.VMEM(w_qkv_fine.shape, bf16),
            pltpu.VMEM((2,) + bias_fine.shape, f32),
            pltpu.VMEM(w_out_fine.shape, bf16),
            pltpu.VMEM(w_merge.shape, bf16),
            pltpu.VMEM(w_qkv_coarse.shape, bf16),
            pltpu.VMEM(bias_coarse.shape, f32),
            pltpu.VMEM(w_out_coarse.shape, bf16),
            pltpu.VMEM(maps.shape, bf16),
            pltpu.VMEM(cmaps.shape, bf16),
            pltpu.VMEM((chunks, 4, 2, HALF_R, HALF_C, LEVELS, D1), bf16),
            pltpu.VMEM((NW * WIN, D1), bf16),
            pltpu.VMEM((NW * WIN, 3 * D1), bf16),
            pltpu.VMEM((NW * WIN, D1), bf16),
            pltpu.VMEM((chunks, 4, 2, HALF_R, HALF_C, LEVELS, D1), bf16),
            pltpu.VMEM(tokens.shape, bf16),
            pltpu.VMEM((CROWS, 4 * D1), bf16),
            pltpu.VMEM((chunks, CROWS, D2), bf16),
            pltpu.VMEM(slots, bf16),
            pltpu.VMEM(slots, bf16),
            pltpu.VMEM((WIN, D2), bf16),
            pltpu.VMEM((WIN, 3 * D2), bf16),
            pltpu.VMEM(slots, bf16),
            pltpu.VMEM(slots, bf16),
            dma((9,)),
            dma((chunks,)),
            dma((chunks,)),
        ]
        + [dma((chunks, 4)) for _ in range(8)],
        compiler_params=pltpu.CompilerParams(
            collective_id=0, has_side_effects=True, vmem_limit_bytes=VMEM_LIMIT
        ),
        name="window_levels",
    )(
        tokens,
        gain_fine[None],
        w_qkv_fine,
        bias_fine,
        w_out_fine,
        gain_merge[None],
        w_merge,
        gain_coarse[None],
        w_qkv_coarse,
        bias_coarse,
        maps,
        cmaps,
        w_out_coarse,
    )
    fine_out = fine_out.reshape(tokens.shape)
    return fine_out.transpose(0, 3, 1, 2, 4), coarse_out.transpose(0, 3, 1, 2, 4)


def solution(mesh):
    tile = P(None, None, "lat", "lon", None)
    return jax.shard_map(
        body,
        mesh=mesh,
        in_specs=(tile,) + (P(),) * 10,
        out_specs=(tile, tile),
        check_vma=False,
    )
```
